256 devices in a mesh: seq: 64 (over x, z, core), rep: 4 (over y).
Axes of the slice: x: 4, y: 4, z: 8, core: 2. Of those that a mesh axis runs over, the one named last changes fastest.
Arguments:
- feats: bfloat16 [262144, 256], P(('rep', 'seq')), parts along dimension 0, may hold values from -6 to 6
- hilbert_rank: int32 [262144], P(('rep', 'seq')), parts along dimension 0, may hold values from 0 to 65535, as said below
- patch_id: int32 [262144], P(('rep', 'seq')), parts along dimension 0, may hold values from 0 to 65535, as said below
- gain: float32 [256], replicated, may hold values from 0.5 to 1.5
- w_qkv: bfloat16 [256, 768], replicated, may hold values from -2.8125 to 2.8125, as said below
- w_out: bfloat16 [256, 256], replicated, may hold values from -1.5 to 1.5
- d_mixed: bfloat16 [262144, 256], P(('rep', 'seq')), parts along dimension 0, may hold values from -6 to 6
Outputs:
- mixed: bfloat16 [262144, 256], P(('rep', 'seq')), parts along dimension 0
- d_feats: bfloat16 [262144, 256], P(('rep', 'seq')), parts along dimension 0
- g_qkv: float32 [1024, 768], P('rep'), parts along dimension 0
- g_out: float32 [1024, 256], P('rep'), parts along dimension 0
- g_gain: float32 [1024], P('rep'), parts along dimension 0
The draws below stay inside these ranges and needn't reach their ends.
There are 4 independent parts, one for each index of `rep`. The reference program is written for one: setup_inputs(seed, part) draws one part's arguments, and reference() takes and returns one part's arrays. A program takes and returns all parts, laid end to end along the dimension named above; an argument that names none is the same for every part. Nothing has to cross between parts.
Inputs may be any that keep to these rules, and one draw needn't show every extreme that they name: A permutation of the points. The owner of a point is hilbert_rank // 1024; of the points of one device at most 4 have any one other device as owner, and in every draw some device sends exactly 4 to some other. `patch_id`: the Hilbert index of the last point of the point's patch, so it never falls along the Hilbert order; patches are the aligned tiles of 1024 points, except that a tile in which a pooled cloud ends is split there into two patches; every patch lies inside one tile, and in every draw some patch fills a whole tile. `w_qkv`: dense real-valued projection.
All inputs are finite; a program needn't handle non-finite values.
Results may differ from the reference program's by a relative error of at most 0.025.
The reference program's roundings to bfloat16 on the way count: a program that leaves them out, or rounds other values in their place, can miss the bound.
Values may be sent and summed in bfloat16 or wider, within the bound.
A program may use at most 64 MiB of HBM per device.

```python
import jax
import jax.numpy as jnp
from jax import lax

C = 256
HDIM = 16
PTS_DEV = 1024
PATCH = 1024
CAP = 4
NPTS = 65536


def draw_hilbert_rank(key, part):
    key = jax.random.fold_in(key, 3)
    keys = jax.random.split(key, 4)
    ndev = NPTS // PTS_DEV
    upper = jnp.triu(jax.random.randint(keys[0], (ndev, ndev), 0, CAP + 1), 1)
    first = jax.random.randint(keys[1], (), 0, ndev - 1)
    index = jnp.arange(ndev)
    forced = (index[:, None] == first) & (index[None, :] == first + 1)
    upper = jnp.where(forced, CAP, upper)
    sends = upper + upper.T
    flows = sends + jnp.diag(PTS_DEV - jnp.sum(sends, axis=1))
    ends = jnp.cumsum(flows, axis=1)
    starts = ends - flows
    arrivals = jnp.cumsum(flows, axis=0) - flows
    shuffle_src = jax.vmap(lambda k: jax.random.permutation(k, PTS_DEV))(jax.random.split(keys[2], ndev))
    place = jnp.argsort(shuffle_src, axis=1)
    owner = jnp.sum((ends[:, None, :] <= place[:, :, None]).astype(jnp.int32), axis=2)
    within = place - jnp.take_along_axis(starts, owner, axis=1)
    offset = jnp.take_along_axis(arrivals, owner, axis=1) + within
    shuffle_dst = jax.vmap(lambda k: jax.random.permutation(k, PTS_DEV))(jax.random.split(keys[3], ndev))
    slot = shuffle_dst[owner, offset]
    return (owner * PTS_DEV + slot).reshape(-1).astype(jnp.int32)


def draw_patch_id(key, part):
    key = jax.random.fold_in(key, 5)
    first, second, third = jax.random.split(key, 3)
    tiles = NPTS // PATCH
    split = jax.random.randint(first, (tiles,), 0, 2) == 1
    where_cut = jax.random.randint(third, (tiles,), 1, PATCH)
    cuts = split[:, None] & (jnp.arange(PATCH)[None, :] == where_cut[:, None])
    whole = jax.random.randint(second, (), 1, tiles)
    cuts = cuts & (jnp.arange(tiles)[:, None] != whole)
    cuts = cuts.at[:, 0].set(True)
    starts = cuts.reshape(-1)
    finals = jnp.concatenate([starts[1:], jnp.ones((1,), dtype=bool)])
    position = jnp.arange(NPTS, dtype=jnp.int32)
    marked = jnp.where(finals, position, NPTS).astype(jnp.int32)
    return lax.cummin(marked, axis=0, reverse=True).astype(jnp.int32)


def draw_w_qkv(key, part):
    key = jax.random.fold_in(key, 7)
    first = jax.random.fold_in(key, 0)
    base = jnp.clip(jax.random.normal(first, (C, 3 * C), jnp.float32), -5.0, 5.0) * C ** (-0.5)
    return base.astype(jnp.bfloat16)


def level_of(key, extent, shards, low, high):
    loudness, own = 1.0, jax.random.fold_in(key, 6)
    for dim, blocks in shards:
        draws = jnp.exp(jax.random.uniform(jax.random.fold_in(own, dim), (blocks,), jnp.float32, low / len(shards), high / len(shards)))
        loudness = loudness * jnp.repeat(draws, extent[dim] // blocks).reshape([-1 if axis == dim else 1 for axis in range(len(extent))])
    return loudness


def scatter_about(own_key, shape, scale, most, cuts=(), held_as=jnp.bfloat16):
    array = scale * jax.random.normal(own_key, shape, jnp.float32)
    if cuts:
        array = array * level_of(own_key, shape, cuts, -0.22, 0.18)
    return jnp.clip(array, -most, most).astype(held_as)


def setup_inputs(seed: int = 0, part: int = 0) -> dict:
    streams_of = jax.random.split(jax.random.key(seed), 8)
    own_keys = jax.random.split(jax.random.fold_in(streams_of[7], part), 8)
    return {
        "feats": scatter_about(own_keys[0], (NPTS, C), 1.0, 6.0, ((0, 64),)),
        "hilbert_rank": draw_hilbert_rank(jax.random.fold_in(jax.random.fold_in(streams_of[7], part), 71), part),
        "patch_id": draw_patch_id(jax.random.fold_in(jax.random.fold_in(streams_of[7], part), 71), part),
        "gain": jnp.clip(1.0 + 0.1 * jax.random.normal(streams_of[3], (C,), jnp.float32), 0.5, 1.5),
        "w_qkv": draw_w_qkv(jax.random.fold_in(streams_of[7], 71), part),
        "w_out": scatter_about(streams_of[5], (C, C), (C // 16) ** -0.5, 1.5),
        "d_mixed": scatter_about(own_keys[6], (NPTS, C), 1.0, 6.0, ((0, 64),)),
    }


eps = 1e-05

def layer_norm(rows):
    wide = rows.astype(jnp.float32)
    center = lax.optimization_barrier(jnp.mean(wide, axis=1, keepdims=True))
    centred = wide - center
    recip = lax.rsqrt(lax.optimization_barrier(jnp.mean(centred * centred, axis=1, keepdims=True)) + eps)
    return (centred * recip, recip)

def tile_attention(qkv_tile, labels, upstream):
    count = qkv_tile.shape[0]
    width = qkv_tile.shape[1] // 3
    heads = width // HDIM
    scale = HDIM ** (-0.5)
    query = qkv_tile[:, :width].reshape(count, heads, HDIM).astype(jnp.float32)
    keys = qkv_tile[:, width:2 * width].reshape(count, heads, HDIM).astype(jnp.float32)
    values = qkv_tile[:, 2 * width:].reshape(count, heads, HDIM).astype(jnp.float32)
    upper = upstream.reshape(count, heads, HDIM).astype(jnp.float32)
    same = labels[:, None] == labels[None, :]
    scores = jnp.einsum('qhd,khd->hqk', query, keys) * scale
    scores = jnp.where(same[None], scores, -1e+30)
    top = lax.optimization_barrier(jnp.max(scores, axis=2, keepdims=True))
    expo = jnp.exp(scores - top)
    probs = expo / lax.optimization_barrier(jnp.sum(expo, axis=2, keepdims=True))
    probs_low = probs.astype(jnp.bfloat16)
    probs_wide = probs_low.astype(jnp.float32)
    attended = jnp.einsum('hqk,khd->qhd', probs_wide, values).reshape(count, width).astype(jnp.bfloat16)
    grad_probs = jnp.einsum('qhd,khd->hqk', upper, values)
    delta = lax.optimization_barrier(jnp.sum(probs * grad_probs, axis=2, keepdims=True))
    grad_scores = (probs * (grad_probs - delta) * scale).astype(jnp.bfloat16).astype(jnp.float32)
    grad_query = jnp.einsum('hqk,khd->qhd', grad_scores, keys).reshape(count, width)
    grad_keys = jnp.einsum('hqk,qhd->khd', grad_scores, query).reshape(count, width)
    grad_values = jnp.einsum('hqk,qhd->khd', probs_wide, upper).reshape(count, width)
    grad_qkv = jnp.concatenate([grad_query, grad_keys, grad_values], axis=1).astype(jnp.bfloat16)
    return (attended, grad_qkv)

def reference(feats, hilbert_rank, patch_id, gain, w_qkv, w_out, d_mixed):
    total = feats.shape[0]
    width = feats.shape[1]
    tiles = total // PATCH
    hilbert = jnp.zeros_like(feats).at[hilbert_rank].set(feats)
    normed, recip = layer_norm(hilbert)
    normed_low = (normed * gain).astype(jnp.bfloat16)
    qkv = jnp.dot(normed_low, w_qkv, preferred_element_type=jnp.float32).astype(jnp.bfloat16)
    grad_att = jnp.dot(d_mixed, w_out.T, preferred_element_type=jnp.float32).astype(jnp.bfloat16)
    attended, grad_qkv = lax.map(lambda pieces: tile_attention(pieces[0], pieces[1], pieces[2]), (qkv.reshape(tiles, PATCH, 3 * width), patch_id.reshape(tiles, PATCH), grad_att.reshape(tiles, PATCH, width)))
    attended = attended.reshape(total, width)
    grad_qkv = grad_qkv.reshape(total, 3 * width)
    mixed = (hilbert.astype(jnp.float32) + jnp.dot(attended, w_out, preferred_element_type=jnp.float32)).astype(jnp.bfloat16)
    g_out = jnp.dot(attended.T, d_mixed, preferred_element_type=jnp.float32)
    g_qkv = jnp.dot(normed_low.T, grad_qkv, preferred_element_type=jnp.float32)
    grad_normed = jnp.dot(grad_qkv, w_qkv.T, preferred_element_type=jnp.float32)
    g_gain = lax.optimization_barrier(jnp.sum(grad_normed * normed, axis=0))
    scaled = grad_normed * gain
    d_norm = recip * (scaled - lax.optimization_barrier(jnp.mean(scaled, axis=1, keepdims=True)) - normed * lax.optimization_barrier(jnp.mean(scaled * normed, axis=1, keepdims=True)))
    d_hilbert = (d_mixed.astype(jnp.float32) + d_norm).astype(jnp.bfloat16)
    d_feats = d_hilbert[hilbert_rank]
    return (mixed, d_feats, g_qkv, g_out, g_gain)
```

```python
import functools

import jax
import jax.numpy as jnp
from jax import lax
from jax.experimental import pallas as pl
from jax.experimental.pallas import tpu as pltpu
from jax.sharding import PartitionSpec as P

F = jnp.float32
B = jnp.bfloat16
I = jnp.int32

N = 1024
C = 256
HDIM = 16
HEADS = C // HDIM
PEERS = 64
CAP = 4
ROWS = 16
CHIPS = 32
PIECE = 32
EPS = 1e-05
MASKED = 1e30
VMEM = 56 << 20

ANYWHERE = pl.BlockSpec(memory_space=pltpu.VMEM)


def dg(a, b, ca, cb):
    return lax.dot_general(a, b, (((ca,), (cb,)), ((), ())), preferred_element_type=F)


def iota(shape, dim):
    return lax.broadcasted_iota(I, shape, dim)


def greet():
    me = lax.axis_index("seq")
    barrier = pltpu.get_barrier_semaphore()

    def signal(step, carry):
        peer = lax.rem(me + step, PEERS)
        pl.semaphore_signal(
            barrier, inc=1, device_id={"seq": peer}, device_id_type=pl.DeviceIdType.MESH
        )
        return carry

    lax.fori_loop(1, PEERS, signal, 0)


def met():
    pl.semaphore_wait(pltpu.get_barrier_semaphore(), PEERS - 1)


def remote(src, dst, send_sem, recv_sem, peer):
    return pltpu.make_async_remote_copy(
        src_ref=src,
        dst_ref=dst,
        send_sem=send_sem,
        recv_sem=recv_sem,
        device_id={"seq": peer},
        device_id_type=pl.DeviceIdType.MESH,
    )


def await_bytes(ref, sem):
    pltpu.make_async_copy(ref, ref, sem).wait()


def exchange(src, dst, send_sem, recv_sem):
    me = lax.axis_index("seq")
    mine = pl.ds(pl.multiple_of(me * ROWS, ROWS), ROWS)

    def send(step, carry):
        peer = lax.rem(me + step, PEERS)
        theirs = pl.ds(pl.multiple_of(peer * ROWS, ROWS), ROWS)
        remote(src.at[theirs], dst.at[mine], send_sem, recv_sem, peer).start()
        return carry

    lax.fori_loop(1, PEERS, send, 0)


def await_exchange(ref, sem):
    await_bytes(ref.at[pl.ds(0, (PEERS - 1) * ROWS)], sem)


def slot_rows(code):
    r = iota((PEERS * ROWS, 1), 0)
    t = r % ROWS
    wanted = jnp.where(t < 3 * CAP, (r // ROWS) * CAP + t % CAP, -2)
    return wanted == code


def pack_kernel(rank_ref, feats_ref, code_ref, got_ref, send, send_sem, recv_sem):
    greet()
    me = lax.axis_index("seq")
    rank = rank_ref[...]
    owner = rank // N
    onehot = (iota((PEERS, N), 0) == owner).astype(F)
    upto = (iota((N, N), 0) <= iota((N, N), 1)).astype(F).astype(B)
    count = jnp.dot(onehot.astype(B), upto, preferred_element_type=F)
    slot = jnp.sum(count * onehot, axis=0, keepdims=True).astype(I) - 1
    code = jnp.where(owner == me, -1, owner * CAP + slot)
    code_ref[...] = code
    chosen = slot_rows(code).astype(F).astype(B)
    place = rank % N
    k = iota((128, N), 0)
    extra = jnp.where(k == 0, place // 32, jnp.where(k == 1, place % 32, jnp.where(k == 2, 1, 0)))
    rows = jnp.dot(chosen, feats_ref[...], preferred_element_type=F)
    places = dg(chosen, extra.astype(F).astype(B), 1, 1)
    t = iota((PEERS * ROWS, 128), 0) % ROWS
    block = jnp.where(t < CAP, rows[:, :128], jnp.where(t < 2 * CAP, rows[:, 128:], places))
    send[...] = block.astype(B)
    got_ref[pl.ds(pl.multiple_of(me * ROWS, ROWS), ROWS), :] = jnp.zeros((ROWS, 128), B)
    met()
    exchange(send, got_ref, send_sem, recv_sem)
    await_exchange(got_ref, recv_sem)
    await_exchange(send, send_sem)


def halves(block, t):
    zero = jnp.zeros_like(block)
    left = jnp.where(t < CAP, block, zero)
    right = jnp.where((t >= CAP) & (t < 2 * CAP), block, zero)
    return jnp.concatenate([left, right], axis=1)


def attention(q_ref, k_ref, v_ref, u_ref, group, att, gq, gk, gv):
    one = jnp.where(group > 0, 1.0, 0.0)
    pad = jnp.zeros((HDIM - 2, N), F)
    q_bias = jnp.concatenate([-MASKED * (1 - one), -MASKED * one, pad], 0).astype(B)
    k_bias = jnp.concatenate([one, 1 - one, pad], 0).astype(B)
    ones = jnp.concatenate([jnp.ones((1, N), F), jnp.zeros((HDIM - 1, N), F)], 0).astype(B)
    scale = HDIM ** (-0.5)

    def head(h, carry):
        rows = pl.ds(pl.multiple_of(h * HDIM, HDIM), HDIM)
        q, k, v, u = q_ref[rows, :], k_ref[rows, :], v_ref[rows, :], u_ref[rows, :]
        qx = jnp.concatenate([q * B(scale), q_bias], 0)
        kx = jnp.concatenate([k, k_bias], 0)
        vx = jnp.concatenate([v, ones], 0)
        scores = dg(kx, qx, 0, 0)
        expo = jnp.exp(scores - jnp.max(scores, axis=0, keepdims=True))
        low = expo.astype(B)
        total = jnp.dot(vx, low, preferred_element_type=F)
        recip = 1.0 / total[HDIM : HDIM + 1]
        attended = total[:HDIM] * recip
        wide = u.astype(F)
        delta = jnp.sum(wide * attended, axis=0, keepdims=True)
        grad_probs = dg(v, u, 0, 0)
        grad_scores = (expo * ((grad_probs - delta) * (recip * scale))).astype(B)
        att[rows, :] = attended.astype(B)
        gq[rows, :] = jnp.dot(k, grad_scores, preferred_element_type=F).astype(B)
        gk[rows, :] = dg(q, grad_scores, 1, 1).astype(B)
        gv[rows, :] = dg((wide * recip).astype(B), low, 1, 1).astype(B)
        return carry

    lax.fori_loop(0, HEADS, head, 0)


def layer_kernel(
    rank_ref, got_ref, feats_ref, patch_ref, gain_ref, w_qkv_ref, w_out_ref, d_mixed_ref,
    mixed_ref, local_ref, back_ref, grads_ref,
    hil, qkv, up, normed, low, att, gqkv, place,
):
    me = lax.axis_index("seq")
    rank = rank_ref[...]
    here = jnp.where(rank // N == me, rank % N, -1)
    got = got_ref[...]
    weight = iota((16, 128), 1)
    weight = jnp.where(weight == 0, 32.0, jnp.where(weight < 2, 1.0, 0.0)).astype(B)
    valid = jnp.where(iota((16, 128), 1) == 2, 1.0, 0.0).astype(B)
    lane = iota((1, N), 1) % ROWS
    at = dg(weight, got, 1, 1)[:1]
    real = dg(valid, got, 1, 1)[:1]
    at = jnp.where(real > 0.5, at, -1.0)
    at = jnp.where(lane < 2 * CAP, -1.0, jnp.where(lane < 3 * CAP, at, -1.0))
    at = jnp.broadcast_to(at, (8, N))
    left = pltpu.roll(at, N - 2 * CAP, 1)[:1]
    right = pltpu.roll(at, N - CAP, 1)[:1]
    at = jnp.where(lane < CAP, left, jnp.where(lane < 2 * CAP, right, -1.0)).astype(I)
    place[...] = jnp.broadcast_to(at, (8, N))
    p = iota((N, 1), 0)
    t = iota((PEERS * ROWS, 128), 0) % ROWS
    stay = (p == here).astype(F).astype(B)
    come = (p == at).astype(F).astype(B)
    rows = jnp.dot(stay, feats_ref[...], preferred_element_type=F)
    rows += jnp.dot(come, halves(got, t), preferred_element_type=F)
    hil[...] = rows.astype(B)

    gain = jnp.broadcast_to(gain_ref[...], (8, C)).T[:, :1]
    wide = rows.T
    centred = wide - jnp.mean(wide, axis=0, keepdims=True)
    recip = lax.rsqrt(jnp.mean(centred * centred, axis=0, keepdims=True) + EPS)
    normed[...] = centred * recip
    low[...] = (normed[...] * gain).astype(B)
    qkv[...] = dg(w_qkv_ref[...], low[...], 0, 0).astype(B)
    up[...] = dg(w_out_ref[...], d_mixed_ref[...], 1, 1).astype(B)

    patch = patch_ref[...]
    attention(
        qkv.at[:C], qkv.at[C : 2 * C], qkv.at[2 * C :], up,
        (patch == patch[:, :1]).astype(F),
        att, gqkv.at[:C], gqkv.at[C : 2 * C], gqkv.at[2 * C :],
    )

    mixed_ref[...] = (hil[...].astype(F) + dg(att[...], w_out_ref[...], 0, 0)).astype(B)
    g_out = jnp.dot(att[...], d_mixed_ref[...], preferred_element_type=F)
    g_qkv = dg(low[...], gqkv[...], 1, 1)
    for j in range(6):
        grads_ref[j * C : (j + 1) * C, :] = g_qkv[:, j * 128 : (j + 1) * 128]
    for j in range(2):
        grads_ref[(6 + j) * C : (7 + j) * C, :] = g_out[:, j * 128 : (j + 1) * 128]

    grad_normed = jnp.dot(w_qkv_ref[...], gqkv[...], preferred_element_type=F)
    scaled = grad_normed * gain
    d_norm = recip * (
        scaled
        - jnp.mean(scaled, axis=0, keepdims=True)
        - normed[...] * jnp.mean(scaled * normed[...], axis=0, keepdims=True)
    )
    d_rows = (d_mixed_ref[...].astype(F).T + d_norm).astype(B)
    stay = (p == here).astype(F).astype(B)
    come = (p == place[:1]).astype(F).astype(B)
    local_ref[...] = jnp.dot(d_rows, stay, preferred_element_type=F).astype(B)
    back = jnp.dot(d_rows, come, preferred_element_type=F)
    back = jnp.where(lane < CAP, back[:128], jnp.where(lane < 2 * CAP, back[128:], 0.0))
    back_ref[...] = back.T.astype(B)


def return_kernel(
    back_ref, grads_ref, ret_ref, sums_ref,
    half_send, half_got, piece_send, piece_got, done,
    row_sems, half_sems, piece_sems, done_sems, last_sems,
):
    greet()
    me = lax.axis_index("seq")
    core = lax.rem(me, 2)
    chip = me // 2
    other = 1 - core
    partner = chip * 2 + other
    half = CHIPS * PIECE

    half_send[...] = grads_ref[pl.ds(pl.multiple_of(other * half, half), half), :].astype(B)
    ret_ref[pl.ds(pl.multiple_of(me * ROWS, ROWS), ROWS), :] = jnp.zeros((ROWS, 128), B)
    met()
    swap = remote(half_send, half_got, half_sems.at[0], half_sems.at[1], partner)
    swap.start()
    exchange(back_ref, ret_ref, row_sems.at[0], row_sems.at[1])
    swap.wait()

    mine = grads_ref[pl.ds(pl.multiple_of(core * half, half), half), :]
    piece_send[...] = (mine + half_got[...].astype(F)).astype(B)
    own = pl.ds(pl.multiple_of(chip * PIECE, PIECE), PIECE)
    piece_got[own, :] = piece_send[own, :]

    def scatter(step, carry):
        to = lax.rem(chip + step, CHIPS)
        theirs = pl.ds(pl.multiple_of(to * PIECE, PIECE), PIECE)
        remote(
            piece_send.at[theirs], piece_got.at[own], piece_sems.at[0], piece_sems.at[1],
            to * 2 + core,
        ).start()
        return carry

    lax.fori_loop(1, CHIPS, scatter, 0)
    others = pl.ds(0, (CHIPS - 1) * PIECE)
    await_bytes(piece_got.at[others], piece_sems.at[1])
    total = piece_got[0:PIECE, :].astype(F)
    for j in range(1, CHIPS):
        total += piece_got[j * PIECE : (j + 1) * PIECE, :].astype(F)
    done[own, :] = total.astype(B)

    def gather(step, carry):
        to = lax.rem(chip + step, CHIPS)
        remote(
            done.at[own], done.at[own], done_sems.at[0], done_sems.at[1], to * 2 + core
        ).start()
        return carry

    lax.fori_loop(1, CHIPS, gather, 0)
    await_bytes(done.at[others], done_sems.at[1])
    here = pl.ds(pl.multiple_of(core * half, half), half)
    last = remote(done, sums_ref.at[here], last_sems.at[0], last_sems.at[1], partner)
    last.start()
    sums_ref[here, :] = done[...]
    await_exchange(ret_ref, row_sems.at[1])
    await_exchange(back_ref, row_sems.at[0])
    await_bytes(piece_send.at[others], piece_sems.at[0])
    await_bytes(done.at[others], done_sems.at[0])
    last.wait()


def finish_kernel(
    code_ref, ret_ref, local_ref, sums_ref, w_qkv_ref, gain_ref,
    d_feats_ref, g_qkv_ref, g_out_ref, g_gain_ref,
):
    t = iota((PEERS * ROWS, 128), 0) % ROWS
    chosen = slot_rows(code_ref[...]).astype(F).astype(B)
    d_feats = dg(halves(ret_ref[...], t), chosen, 0, 0) + local_ref[...].astype(F)
    d_feats_ref[...] = d_feats.T.astype(B)
    total = jnp.zeros((C, 128), F)
    for j in range(6):
        part = sums_ref[j * C : (j + 1) * C, :].astype(F)
        g_qkv_ref[:, j * 128 : (j + 1) * 128] = part
        total += part * w_qkv_ref[:, j * 128 : (j + 1) * 128].astype(F)
    for j in range(2):
        g_out_ref[:, j * 128 : (j + 1) * 128] = sums_ref[(6 + j) * C : (7 + j) * C, :].astype(F)
    g_gain_ref[...] = jnp.sum(total.T, axis=0, keepdims=True) / gain_ref[...]


def call(kernel, out_shapes, n_in, scratch=(), collective_id=None):
    params = dict(vmem_limit_bytes=VMEM)
    if collective_id is not None:
        params.update(collective_id=collective_id, has_side_effects=True)
    return pl.pallas_call(
        kernel,
        out_shape=[jax.ShapeDtypeStruct(s, d) for s, d in out_shapes],
        in_specs=[ANYWHERE] * n_in,
        out_specs=[ANYWHERE] * len(out_shapes),
        scratch_shapes=list(scratch),
        compiler_params=pltpu.CompilerParams(**params),
    )


def on_device(feats, hilbert_rank, patch_id, gain, w_qkv, w_out, d_mixed):
    rank = hilbert_rank.reshape(1, N)
    patch = patch_id.reshape(1, N)
    gain = gain.reshape(1, C)
    blocks = (PEERS * ROWS, 128)
    dma = pltpu.SemaphoreType.DMA
    code, got = call(
        pack_kernel, [((1, N), I), (blocks, B)], 2,
        [pltpu.VMEM(blocks, B), dma, dma], collective_id=0,
    )(rank, feats)
    mixed, local, back, grads = call(
        layer_kernel, [((N, C), B), ((C, N), B), (blocks, B), ((8 * C, 128), F)], 8,
        [
            pltpu.VMEM((N, C), B), pltpu.VMEM((3 * C, N), B), pltpu.VMEM((C, N), B),
            pltpu.VMEM((C, N), F), pltpu.VMEM((C, N), B), pltpu.VMEM((C, N), B),
            pltpu.VMEM((3 * C, N), B), pltpu.VMEM((8, N), I),
        ],
    )(rank, got, feats, patch, gain, w_qkv, w_out, d_mixed)
    half = (CHIPS * PIECE, 128)
    ret, sums = call(
        return_kernel, [(blocks, B), ((8 * C, 128), B)], 2,
        [pltpu.VMEM(half, B)] * 5 + [dma((2,))] * 5, collective_id=1,
    )(back, grads)
    d_feats, g_qkv, g_out, g_gain = call(
        finish_kernel, [((N, C), B), ((C, 3 * C), F), ((C, C), F), ((1, C), F)], 6
    )(code, ret, local, sums, w_qkv, gain)
    return (mixed, d_feats, g_qkv, g_out, g_gain.reshape(C))


def solution(mesh):
    return jax.shard_map(
        on_device,
        mesh=mesh,
        in_specs=(
            P(("rep", "seq"), None),
            P(("rep", "seq")),
            P(("rep", "seq")),
            P(),
            P(),
            P(),
            P(("rep", "seq"), None),
        ),
        out_specs=(
            P(("rep", "seq"), None),
            P(("rep", "seq"), None),
            P("rep", None),
            P("rep", None),
            P("rep"),
        ),
        check_vma=False,
    )
```

```python
import functools

import jax
import jax.numpy as jnp
from jax import lax
from jax.experimental import pallas as pl
from jax.experimental.pallas import tpu as pltpu
from jax.sharding import PartitionSpec as P

F = jnp.float32
B = jnp.bfloat16
I = jnp.int32

N = 1024
C = 256
HDIM = 16
HEADS = C // HDIM
PEERS = 64
CAP = 4
ROWS = 16
CHIPS = 32
GROUPS = 2
WIDE = C // GROUPS
PIECE = 16
HALF = CHIPS * PIECE
EPS = 1e-05
MASKED = 1e30
VMEM = 56 << 20

ANYWHERE = pl.BlockSpec(memory_space=pltpu.VMEM)


def dg(a, b, ca, cb):
    return lax.dot_general(a, b, (((ca,), (cb,)), ((), ())), preferred_element_type=F)


def iota(shape, dim):
    return lax.broadcasted_iota(I, shape, dim)


def greet():
    me = lax.axis_index("seq")
    barrier = pltpu.get_barrier_semaphore()

    def signal(step, carry):
        peer = lax.rem(me + step, PEERS)
        pl.semaphore_signal(
            barrier, inc=1, device_id={"seq": peer}, device_id_type=pl.DeviceIdType.MESH
        )
        return carry

    lax.fori_loop(1, PEERS, signal, 0)


def met():
    pl.semaphore_wait(pltpu.get_barrier_semaphore(), PEERS - 1)


def remote(src, dst, send_sem, recv_sem, peer):
    return pltpu.make_async_remote_copy(
        src_ref=src,
        dst_ref=dst,
        send_sem=send_sem,
        recv_sem=recv_sem,
        device_id={"seq": peer},
        device_id_type=pl.DeviceIdType.MESH,
    )


def await_bytes(ref, sem):
    pltpu.make_async_copy(ref, ref, sem).wait()


def exchange(src, dst, send_sem, recv_sem):
    me = lax.axis_index("seq")
    mine = pl.ds(pl.multiple_of(me * ROWS, ROWS), ROWS)

    def send(step, carry):
        peer = lax.rem(me + step, PEERS)
        theirs = pl.ds(pl.multiple_of(peer * ROWS, ROWS), ROWS)
        remote(src.at[theirs], dst.at[mine], send_sem, recv_sem, peer).start()
        return carry

    lax.fori_loop(1, PEERS, send, 0)


def await_exchange(ref, sem):
    await_bytes(ref.at[pl.ds(0, (PEERS - 1) * ROWS)], sem)


def slot_rows(code):
    r = iota((PEERS * ROWS, 1), 0)
    t = r % ROWS
    wanted = jnp.where(t < 3 * CAP, (r // ROWS) * CAP + t % CAP, -2)
    return wanted == code


def halves(block, t):
    zero = jnp.zeros_like(block)
    left = jnp.where(t < CAP, block, zero)
    right = jnp.where((t >= CAP) & (t < 2 * CAP), block, zero)
    return jnp.concatenate([left, right], axis=1)


def attention(q_ref, k_ref, v_ref, u_ref, group, att, gq, gk, gv, after):
    one = jnp.where(group > 0, 1.0, 0.0)
    pad = jnp.zeros((HDIM - 2, N), F)
    q_bias = jnp.concatenate([-MASKED * (1 - one), -MASKED * one, pad], 0).astype(B)
    k_bias = jnp.concatenate([one, 1 - one, pad], 0).astype(B)
    ones = jnp.concatenate([jnp.ones((1, N), F), jnp.zeros((HDIM - 1, N), F)], 0).astype(B)
    scale = HDIM ** (-0.5)

    def head(h, carry):
        rows = pl.ds(pl.multiple_of(h * HDIM, HDIM), HDIM)
        q, k, v, u = q_ref[rows, :], k_ref[rows, :], v_ref[rows, :], u_ref[rows, :]
        qx = jnp.concatenate([q * B(scale), q_bias], 0)
        kx = jnp.concatenate([k, k_bias], 0)
        vx = jnp.concatenate([v, ones], 0)
        scores = dg(kx, qx, 0, 0)
        expo = jnp.exp(scores - jnp.max(scores, axis=0, keepdims=True))
        low = expo.astype(B)
        total = jnp.dot(vx, low, preferred_element_type=F)
        recip = 1.0 / total[HDIM : HDIM + 1]
        attended = total[:HDIM] * recip
        wide = u.astype(F)
        delta = jnp.sum(wide * attended, axis=0, keepdims=True)
        grad_probs = dg(v, u, 0, 0)
        grad_scores = (expo * ((grad_probs - delta) * (recip * scale))).astype(B)
        att[rows, :] = attended.astype(B)
        gq[rows, :] = jnp.dot(k, grad_scores, preferred_element_type=F).astype(B)
        gk[rows, :] = dg(q, grad_scores, 1, 1).astype(B)
        gv[rows, :] = dg((wide * recip).astype(B), low, 1, 1).astype(B)
        after(h)
        return carry

    lax.fori_loop(0, HEADS, head, 0)


def layer_kernel(
    rank_ref, feats_ref, patch_ref, gain_ref, w_qkv_ref, w_out_ref, d_mixed_ref,
    code_ref, mixed_ref, local_ref, ret_ref, sums_ref,
    send, got, hil, qkv, up, normed, low, low_rows, att, gqkv, chunk,
    half_send, half_got, piece_send, piece_got, done,
    go_sems, back_sems, half_sems, piece_sems, done_sems, last_sems,
):
    greet()
    me = lax.axis_index("seq")
    core = lax.rem(me, 2)
    chip = me // 2
    partner = chip * 2 + 1 - core
    own = pl.ds(pl.multiple_of(chip * PIECE, PIECE), PIECE)
    others = pl.ds(0, (CHIPS - 1) * PIECE)

    rank = rank_ref[...]
    owner = rank // N
    onehot = (iota((PEERS, N), 0) == owner).astype(F)
    upto = (iota((N, N), 0) <= iota((N, N), 1)).astype(F).astype(B)
    count = jnp.dot(onehot.astype(B), upto, preferred_element_type=F)
    slot = jnp.sum(count * onehot, axis=0, keepdims=True).astype(I) - 1
    code = jnp.where(owner == me, -1, owner * CAP + slot)
    code_ref[...] = code
    chosen = slot_rows(code).astype(F).astype(B)
    spot = rank % N
    k = iota((128, N), 0)
    extra = jnp.where(k == 0, spot // 32, jnp.where(k == 1, spot % 32, jnp.where(k == 2, 1, 0)))
    rows = jnp.dot(chosen, feats_ref[...], preferred_element_type=F)
    spots = dg(chosen, extra.astype(F).astype(B), 1, 1)
    t = iota((PEERS * ROWS, 128), 0) % ROWS
    block = jnp.where(t < CAP, rows[:, :128], jnp.where(t < 2 * CAP, rows[:, 128:], spots))
    send[...] = block.astype(B)
    mine = pl.ds(pl.multiple_of(me * ROWS, ROWS), ROWS)
    got[mine, :] = jnp.zeros((ROWS, 128), B)
    ret_ref[mine, :] = jnp.zeros((ROWS, 128), B)
    met()
    exchange(send, got, go_sems.at[0], go_sems.at[1])

    here = jnp.where(owner == me, spot, -1)
    p = iota((N, 1), 0)
    stay = (p == here).astype(F).astype(B)
    hil[...] = jnp.dot(stay, feats_ref[...], preferred_element_type=F).astype(B)
    up[...] = dg(w_out_ref[...], d_mixed_ref[...], 1, 1).astype(B)
    gain = jnp.broadcast_to(gain_ref[...], (8, C)).T[:, :1]
    await_exchange(got, go_sems.at[1])
    await_exchange(send, go_sems.at[0])

    arrived = got[...]
    weight = iota((16, 128), 1)
    weight = jnp.where(weight == 0, 32.0, jnp.where(weight < 2, 1.0, 0.0)).astype(B)
    valid = jnp.where(iota((16, 128), 1) == 2, 1.0, 0.0).astype(B)
    lane = iota((1, N), 1) % ROWS
    at = dg(weight, arrived, 1, 1)[:1]
    real = dg(valid, arrived, 1, 1)[:1]
    at = jnp.where(real > 0.5, at, -1.0)
    at = jnp.where(lane < 2 * CAP, -1.0, jnp.where(lane < 3 * CAP, at, -1.0))
    at = jnp.broadcast_to(at, (8, N))
    left = pltpu.roll(at, N - 2 * CAP, 1)[:1]
    right = pltpu.roll(at, N - CAP, 1)[:1]
    at = jnp.where(lane < CAP, left, jnp.where(lane < 2 * CAP, right, -1.0)).astype(I)
    come = (p == at).astype(F).astype(B)
    rows = hil[...].astype(F) + jnp.dot(come, halves(arrived, t), preferred_element_type=F)
    hil[...] = rows.astype(B)

    wide = rows.T
    centred = wide - jnp.mean(wide, axis=0, keepdims=True)
    recip = lax.rsqrt(jnp.mean(centred * centred, axis=0, keepdims=True) + EPS)
    normed[...] = centred * recip
    scaled = normed[...] * gain
    low[...] = scaled.astype(B)
    low_rows[...] = scaled.T.astype(B)
    qkv[...] = dg(w_qkv_ref[...], low[...], 0, 0).astype(B)

    def start_sum(g):
        span = slice(g * WIDE, (g + 1) * WIDE)
        parts = [gqkv[m * C + g * WIDE : m * C + (g + 1) * WIDE, :] for m in range(3)]
        sums = [jnp.dot(part, low_rows[...], preferred_element_type=F) for part in parts]
        sums.append(jnp.dot(att[span, :], d_mixed_ref[...], preferred_element_type=F))
        for m in range(4):
            for side in range(2):
                first = (m // 2) * HALF + side * 2 * WIDE + (m % 2) * WIDE
                chunk[first : first + WIDE, :] = sums[m][:, side * 128 : (side + 1) * 128]
        theirs = pl.ds(pl.multiple_of((1 - core) * HALF, HALF), HALF)
        half_send[g] = chunk[theirs, :].astype(B)
        remote(
            half_send.at[g], half_got.at[g], half_sems.at[g, 0], half_sems.at[g, 1], partner
        ).start()

    def scatter_sum(g):
        await_bytes(half_got.at[g], half_sems.at[g, 1])
        kept = chunk[pl.ds(pl.multiple_of(core * HALF, HALF), HALF), :]
        piece_send[g] = (kept + half_got[g].astype(F)).astype(B)
        piece_got[g, own, :] = piece_send[g, own, :]

        def scatter(step, carry):
            to = lax.rem(chip + step, CHIPS)
            theirs = pl.ds(pl.multiple_of(to * PIECE, PIECE), PIECE)
            remote(
                piece_send.at[g, theirs], piece_got.at[g, own],
                piece_sems.at[g, 0], piece_sems.at[g, 1], to * 2 + core,
            ).start()
            return carry

        lax.fori_loop(1, CHIPS, scatter, 0)

    def gather_sum(g):
        await_bytes(piece_got.at[g, others], piece_sems.at[g, 1])
        total = piece_got[g, 0:PIECE, :].astype(F)
        for j in range(1, CHIPS):
            total += piece_got[g, j * PIECE : (j + 1) * PIECE, :].astype(F)
        done[g, own, :] = total.astype(B)

        def gather(step, carry):
            to = lax.rem(chip + step, CHIPS)
            remote(
                done.at[g, own], done.at[g, own],
                done_sems.at[g, 0], done_sems.at[g, 1], to * 2 + core,
            ).start()
            return carry

        lax.fori_loop(1, CHIPS, gather, 0)

    def kept_half(g):
        return pl.ds(pl.multiple_of(g * 2 * HALF + core * HALF, HALF), HALF)

    def share_sum(g):
        await_bytes(done.at[g, others], done_sems.at[g, 1])
        remote(
            done.at[g], sums_ref.at[kept_half(g)], last_sems.at[g, 0], last_sems.at[g, 1], partner
        ).start()
        sums_ref[kept_half(g), :] = done[g]

    def end_sum(g):
        await_bytes(done.at[g], last_sems.at[g, 1])
        await_bytes(done.at[g], last_sems.at[g, 0])
        await_bytes(half_send.at[g], half_sems.at[g, 0])
        await_bytes(piece_send.at[g, others], piece_sems.at[g, 0])
        await_bytes(done.at[g, others], done_sems.at[g, 0])

    def after(h):
        per = HEADS // GROUPS
        for k, stage in enumerate((start_sum, scatter_sum, gather_sum, share_sum)):
            pl.when(h == per - 1 + 2 * k)(functools.partial(stage, 0))

    patch = patch_ref[...]
    attention(
        qkv.at[:C], qkv.at[C : 2 * C], qkv.at[2 * C :], up,
        (patch == patch[:, :1]).astype(F),
        att, gqkv.at[:C], gqkv.at[C : 2 * C], gqkv.at[2 * C :], after,
    )
    start_sum(1)

    grad_normed = jnp.dot(w_qkv_ref[...], gqkv[...], preferred_element_type=F)
    scaled = grad_normed * gain
    d_norm = recip * (
        scaled
        - jnp.mean(scaled, axis=0, keepdims=True)
        - normed[...] * jnp.mean(scaled * normed[...], axis=0, keepdims=True)
    )
    d_rows = (d_mixed_ref[...].astype(F).T + d_norm).astype(B)
    come = (p == at).astype(F).astype(B)
    back = jnp.dot(d_rows, come, preferred_element_type=F)
    back = jnp.where(lane < CAP, back[:128], jnp.where(lane < 2 * CAP, back[128:], 0.0))
    send[...] = back.T.astype(B)
    exchange(send, ret_ref, back_sems.at[0], back_sems.at[1])
    scatter_sum(1)
    stay = (p == here).astype(F).astype(B)
    local_ref[...] = jnp.dot(d_rows, stay, preferred_element_type=F).astype(B)
    mixed_ref[...] = (hil[...].astype(F) + dg(att[...], w_out_ref[...], 0, 0)).astype(B)
    gather_sum(1)
    await_exchange(ret_ref, back_sems.at[1])
    await_exchange(send, back_sems.at[0])
    share_sum(1)
    end_sum(0)
    end_sum(1)


def finish_kernel(
    code_ref, ret_ref, local_ref, sums_ref, w_qkv_ref, gain_ref,
    d_feats_ref, g_qkv_ref, g_out_ref, g_gain_ref,
):
    t = iota((PEERS * ROWS, 128), 0) % ROWS
    chosen = slot_rows(code_ref[...]).astype(F).astype(B)
    d_feats = dg(halves(ret_ref[...], t), chosen, 0, 0) + local_ref[...].astype(F)
    d_feats_ref[...] = d_feats.T.astype(B)
    for side in range(2):
        lanes = slice(side * 128, (side + 1) * 128)
        column = jnp.zeros((128, 128), F)
        for g in range(GROUPS):
            for m in range(4):
                first = (2 * g + m // 2) * HALF + side * 2 * WIDE + (m % 2) * WIDE
                part = sums_ref[first : first + WIDE, :].astype(F)
                if m < 3:
                    at = slice(m * C + g * WIDE, m * C + (g + 1) * WIDE)
                    part = part.T
                    g_qkv_ref[lanes, at] = part
                    column += part * w_qkv_ref[lanes, at].astype(F)
                else:
                    g_out_ref[g * WIDE : (g + 1) * WIDE, lanes] = part
        total_row = jnp.sum(column.T, axis=0, keepdims=True)
        g_gain_ref[:, lanes] = total_row / gain_ref[:, lanes]


def call(kernel, out_shapes, n_in, scratch=(), collective_id=None):
    params = dict(vmem_limit_bytes=VMEM)
    if collective_id is not None:
        params.update(collective_id=collective_id, has_side_effects=True)
    return pl.pallas_call(
        kernel,
        out_shape=[jax.ShapeDtypeStruct(s, d) for s, d in out_shapes],
        in_specs=[ANYWHERE] * n_in,
        out_specs=[ANYWHERE] * len(out_shapes),
        scratch_shapes=list(scratch),
        compiler_params=pltpu.CompilerParams(**params),
    )


def on_device(feats, hilbert_rank, patch_id, gain, w_qkv, w_out, d_mixed):
    rank = hilbert_rank.reshape(1, N)
    patch = patch_id.reshape(1, N)
    gain = gain.reshape(1, C)
    blocks = (PEERS * ROWS, 128)
    sums_shape = (GROUPS * 2 * HALF, 128)
    dma = pltpu.SemaphoreType.DMA
    by_point, by_channel = (N, C), (C, N)
    code, mixed, local, ret, sums = call(
        layer_kernel,
        [((1, N), I), (by_point, B), (by_channel, B), (blocks, B), (sums_shape, B)],
        7,
        [
            pltpu.VMEM(blocks, B), pltpu.VMEM(blocks, B), pltpu.VMEM(by_point, B),
            pltpu.VMEM((3 * C, N), B), pltpu.VMEM(by_channel, B), pltpu.VMEM(by_channel, F),
            pltpu.VMEM(by_channel, B), pltpu.VMEM(by_point, B), pltpu.VMEM(by_channel, B),
            pltpu.VMEM((3 * C, N), B), pltpu.VMEM((2 * HALF, 128), F),
        ]
        + [pltpu.VMEM((GROUPS, HALF, 128), B)] * 5
        + [dma((2,))] * 2
        + [dma((GROUPS, 2))] * 4,
        collective_id=0,
    )(rank, feats, patch, gain, w_qkv, w_out, d_mixed)
    d_feats, g_qkv, g_out, g_gain = call(
        finish_kernel, [((N, C), B), ((C, 3 * C), F), ((C, C), F), ((1, C), F)], 6
    )(code, ret, local, sums, w_qkv, gain)
    return (mixed, d_feats, g_qkv, g_out, g_gain.reshape(C))


def solution(mesh):
    return jax.shard_map(
        on_device,
        mesh=mesh,
        in_specs=(
            P(("rep", "seq"), None),
            P(("rep", "seq")),
            P(("rep", "seq")),
            P(),
            P(),
            P(),
            P(("rep", "seq"), None),
        ),
        out_specs=(
            P(("rep", "seq"), None),
            P(("rep", "seq"), None),
            P("rep", None),
            P("rep", None),
            P("rep"),
        ),
        check_vma=False,
    )
```

```python
import functools

import jax
import jax.numpy as jnp
from jax import lax
from jax.experimental import pallas as pl
from jax.experimental.pallas import tpu as pltpu
from jax.sharding import PartitionSpec as P

F = jnp.float32
B = jnp.bfloat16
I = jnp.int32

N = 1024
C = 256
HDIM = 16
HEADS = C // HDIM
PEERS = 64
CAP = 4
ROWS = 16
CHIPS = 32
GROUPS = 2
WIDE = C // GROUPS
PIECE = 16
HALF = CHIPS * PIECE
EPS = 1e-05
MASKED = 1e30
LOG2E = 1.4426950408889634
UNROLL = 2
VMEM = 56 << 20

ANYWHERE = pl.BlockSpec(memory_space=pltpu.VMEM)


def dg(a, b, ca, cb):
    return lax.dot_general(a, b, (((ca,), (cb,)), ((), ())), preferred_element_type=F)


def iota(shape, dim):
    return lax.broadcasted_iota(I, shape, dim)


def greet():
    me = lax.axis_index("seq")
    barrier = pltpu.get_barrier_semaphore()

    def signal(step, carry):
        peer = lax.rem(me + step, PEERS)
        pl.semaphore_signal(
            barrier, inc=1, device_id={"seq": peer}, device_id_type=pl.DeviceIdType.MESH
        )
        return carry

    lax.fori_loop(1, PEERS, signal, 0)


def met():
    pl.semaphore_wait(pltpu.get_barrier_semaphore(), PEERS - 1)


def remote(src, dst, send_sem, recv_sem, peer):
    return pltpu.make_async_remote_copy(
        src_ref=src,
        dst_ref=dst,
        send_sem=send_sem,
        recv_sem=recv_sem,
        device_id={"seq": peer},
        device_id_type=pl.DeviceIdType.MESH,
    )


def await_bytes(ref, sem):
    pltpu.make_async_copy(ref, ref, sem).wait()


def exchange(src, dst, send_sem, recv_sem):
    me = lax.axis_index("seq")
    mine = pl.ds(pl.multiple_of(me * ROWS, ROWS), ROWS)

    def send(step, carry):
        peer = lax.rem(me + step, PEERS)
        theirs = pl.ds(pl.multiple_of(peer * ROWS, ROWS), ROWS)
        remote(src.at[theirs], dst.at[mine], send_sem, recv_sem, peer).start()
        return carry

    lax.fori_loop(1, PEERS, send, 0)


def await_exchange(ref, sem):
    await_bytes(ref.at[pl.ds(0, (PEERS - 1) * ROWS)], sem)


def slot_rows(code):
    r = iota((PEERS * ROWS, 1), 0)
    t = r % ROWS
    wanted = jnp.where(t < 3 * CAP, (r // ROWS) * CAP + t % CAP, -2)
    return wanted == code


def halves(block, t):
    zero = jnp.zeros_like(block)
    left = jnp.where(t < CAP, block, zero)
    right = jnp.where((t >= CAP) & (t < 2 * CAP), block, zero)
    return jnp.concatenate([left, right], axis=1)


def split(x):
    high = x.astype(B)
    return high, (x - high.astype(F)).astype(B)


def attention(q_ref, k_ref, v_ref, u_ref, group, att, gq, gk, gv, after):
    one = jnp.where(group > 0, 1.0, 0.0)
    pad = jnp.zeros((HDIM - 2, N), F)
    q_bias = jnp.concatenate([-MASKED * (1 - one), -MASKED * one, pad], 0).astype(B)
    k_bias = jnp.concatenate([one, 1 - one, pad], 0).astype(B)
    ones = jnp.concatenate([jnp.ones((1, N), F), jnp.zeros((HDIM - 1, N), F)], 0).astype(B)
    scale = HDIM ** (-0.5)

    def head(h):
        rows = pl.ds(pl.multiple_of(h * HDIM, HDIM), HDIM)
        q, k, v = q_ref[rows, :], k_ref[rows, :], v_ref[rows, :]
        q_wide, k_wide, v_wide = q.astype(F), k.astype(F), v.astype(F)
        u = u_ref[rows, :].astype(F)
        center = jnp.mean(v_wide, axis=1, keepdims=True)
        v_wide = v_wide - center
        q_high, q_low = split(q_wide * (scale * LOG2E))
        scores = dg(
            jnp.concatenate([k, k, k_bias], 0), jnp.concatenate([q_high, q_low, q_bias], 0), 0, 0
        )
        low = jnp.exp2(scores - jnp.max(scores, axis=0, keepdims=True)).astype(B)
        left = [v, ones, k] + [(v_wide[a : a + 1] * k_wide).astype(B) for a in range(HDIM)]
        sums = jnp.dot(jnp.concatenate(left, 0), low, preferred_element_type=F)
        recip = 1.0 / sums[HDIM : HDIM + 1]
        attended = sums[:HDIM] * recip
        delta = jnp.sum(u * (attended - center), axis=0, keepdims=True)
        grad = -delta * sums[2 * HDIM : 3 * HDIM]
        for a in range(HDIM):
            grad += u[a : a + 1] * sums[(3 + a) * HDIM : (4 + a) * HDIM]
        att[rows, :] = attended.astype(B)
        gq[rows, :] = (grad * (recip * scale)).astype(B)
        u = u * recip
        q_wide = q_wide * scale
        left = [u.astype(B), (q_wide * (-delta * recip)).astype(B)]
        left += [(u[a : a + 1] * q_wide).astype(B) for a in range(HDIM)]
        sums = dg(jnp.concatenate(left, 0), low, 1, 1)
        grad = sums[HDIM : 2 * HDIM]
        for a in range(HDIM):
            grad += v_wide[a : a + 1] * sums[(2 + a) * HDIM : (3 + a) * HDIM]
        gv[rows, :] = sums[:HDIM].astype(B)
        gk[rows, :] = grad.astype(B)

    def heads(i, carry):
        for j in range(UNROLL):
            head(i * UNROLL + j)
        after(i * UNROLL + UNROLL - 1)
        return carry

    lax.fori_loop(0, HEADS // UNROLL, heads, 0)


def layer_kernel(
    rank_ref, feats_ref, patch_ref, gain_ref, w_qkv_ref, w_out_ref, d_mixed_ref,
    code_ref, mixed_ref, local_ref, ret_ref, sums_ref,
    send, got, hil, qkv, up, normed, low, low_rows, att, gqkv, chunk,
    half_send, half_got, piece_send, piece_got, done,
    go_sems, back_sems, half_sems, piece_sems, done_sems, last_sems,
):
    greet()
    me = lax.axis_index("seq")
    core = lax.rem(me, 2)
    chip = me // 2
    partner = chip * 2 + 1 - core
    own = pl.ds(pl.multiple_of(chip * PIECE, PIECE), PIECE)
    others = pl.ds(0, (CHIPS - 1) * PIECE)

    rank = rank_ref[...]
    owner = rank // N
    onehot = (iota((PEERS, N), 0) == owner).astype(F)
    upto = (iota((N, N), 0) <= iota((N, N), 1)).astype(F).astype(B)
    count = jnp.dot(onehot.astype(B), upto, preferred_element_type=F)
    slot = jnp.sum(count * onehot, axis=0, keepdims=True).astype(I) - 1
    code = jnp.where(owner == me, -1, owner * CAP + slot)
    code_ref[...] = code
    chosen = slot_rows(code).astype(F).astype(B)
    spot = rank % N
    k = iota((128, N), 0)
    extra = jnp.where(k == 0, spot // 32, jnp.where(k == 1, spot % 32, jnp.where(k == 2, 1, 0)))
    rows = jnp.dot(chosen, feats_ref[...], preferred_element_type=F)
    spots = dg(chosen, extra.astype(F).astype(B), 1, 1)
    t = iota((PEERS * ROWS, 128), 0) % ROWS
    block = jnp.where(t < CAP, rows[:, :128], jnp.where(t < 2 * CAP, rows[:, 128:], spots))
    send[...] = block.astype(B)
    mine = pl.ds(pl.multiple_of(me * ROWS, ROWS), ROWS)
    got[mine, :] = jnp.zeros((ROWS, 128), B)
    ret_ref[mine, :] = jnp.zeros((ROWS, 128), B)
    met()
    exchange(send, got, go_sems.at[0], go_sems.at[1])

    here = jnp.where(owner == me, spot, -1)
    p = iota((N, 1), 0)
    stay = (p == here).astype(F).astype(B)
    hil[...] = jnp.dot(stay, feats_ref[...], preferred_element_type=F).astype(B)
    up[...] = dg(w_out_ref[...], d_mixed_ref[...], 1, 1).astype(B)
    gain = jnp.broadcast_to(gain_ref[...], (8, C)).T[:, :1]
    await_exchange(got, go_sems.at[1])
    await_exchange(send, go_sems.at[0])

    arrived = got[...]
    weight = iota((16, 128), 1)
    weight = jnp.where(weight == 0, 32.0, jnp.where(weight < 2, 1.0, 0.0)).astype(B)
    valid = jnp.where(iota((16, 128), 1) == 2, 1.0, 0.0).astype(B)
    lane = iota((1, N), 1) % ROWS
    at = dg(weight, arrived, 1, 1)[:1]
    real = dg(valid, arrived, 1, 1)[:1]
    at = jnp.where(real > 0.5, at, -1.0)
    at = jnp.where(lane < 2 * CAP, -1.0, jnp.where(lane < 3 * CAP, at, -1.0))
    at = jnp.broadcast_to(at, (8, N))
    left = pltpu.roll(at, N - 2 * CAP, 1)[:1]
    right = pltpu.roll(at, N - CAP, 1)[:1]
    at = jnp.where(lane < CAP, left, jnp.where(lane < 2 * CAP, right, -1.0)).astype(I)
    come = (p == at).astype(F).astype(B)
    rows = hil[...].astype(F) + jnp.dot(come, halves(arrived, t), preferred_element_type=F)
    hil[...] = rows.astype(B)

    wide = rows.T
    centred = wide - jnp.mean(wide, axis=0, keepdims=True)
    recip = lax.rsqrt(jnp.mean(centred * centred, axis=0, keepdims=True) + EPS)
    normed[...] = centred * recip
    scaled = normed[...] * gain
    low[...] = scaled.astype(B)
    low_rows[...] = scaled.T.astype(B)
    qkv[...] = dg(w_qkv_ref[...], low[...], 0, 0).astype(B)

    def start_sum(g):
        span = slice(g * WIDE, (g + 1) * WIDE)
        parts = [gqkv[m * C + g * WIDE : m * C + (g + 1) * WIDE, :] for m in range(3)]
        sums = [jnp.dot(part, low_rows[...], preferred_element_type=F) for part in parts]
        sums.append(jnp.dot(att[span, :], d_mixed_ref[...], preferred_element_type=F))
        for m in range(4):
            for side in range(2):
                first = (m // 2) * HALF + side * 2 * WIDE + (m % 2) * WIDE
                chunk[first : first + WIDE, :] = sums[m][:, side * 128 : (side + 1) * 128]
        theirs = pl.ds(pl.multiple_of((1 - core) * HALF, HALF), HALF)
        half_send[g] = chunk[theirs, :].astype(B)
        remote(
            half_send.at[g], half_got.at[g], half_sems.at[g, 0], half_sems.at[g, 1], partner
        ).start()

    def scatter_sum(g):
        await_bytes(half_got.at[g], half_sems.at[g, 1])
        kept = chunk[pl.ds(pl.multiple_of(core * HALF, HALF), HALF), :]
        piece_send[g] = (kept + half_got[g].astype(F)).astype(B)
        piece_got[g, own, :] = piece_send[g, own, :]

        def scatter(step, carry):
            to = lax.rem(chip + step, CHIPS)
            theirs = pl.ds(pl.multiple_of(to * PIECE, PIECE), PIECE)
            remote(
                piece_send.at[g, theirs], piece_got.at[g, own],
                piece_sems.at[g, 0], piece_sems.at[g, 1], to * 2 + core,
            ).start()
            return carry

        lax.fori_loop(1, CHIPS, scatter, 0)

    def gather_sum(g):
        await_bytes(piece_got.at[g, others], piece_sems.at[g, 1])
        total = piece_got[g, 0:PIECE, :].astype(F)
        for j in range(1, CHIPS):
            total += piece_got[g, j * PIECE : (j + 1) * PIECE, :].astype(F)
        done[g, own, :] = total.astype(B)

        def gather(step, carry):
            to = lax.rem(chip + step, CHIPS)
            remote(
                done.at[g, own], done.at[g, own],
                done_sems.at[g, 0], done_sems.at[g, 1], to * 2 + core,
            ).start()
            return carry

        lax.fori_loop(1, CHIPS, gather, 0)

    def kept_half(g):
        return pl.ds(pl.multiple_of(g * 2 * HALF + core * HALF, HALF), HALF)

    def share_sum(g):
        await_bytes(done.at[g, others], done_sems.at[g, 1])
        remote(
            done.at[g], sums_ref.at[kept_half(g)], last_sems.at[g, 0], last_sems.at[g, 1], partner
        ).start()
        sums_ref[kept_half(g), :] = done[g]

    def end_sum(g):
        await_bytes(done.at[g], last_sems.at[g, 1])
        await_bytes(done.at[g], last_sems.at[g, 0])
        await_bytes(half_send.at[g], half_sems.at[g, 0])
        await_bytes(piece_send.at[g, others], piece_sems.at[g, 0])
        await_bytes(done.at[g, others], done_sems.at[g, 0])

    def after(h):
        per = HEADS // GROUPS
        for k, stage in enumerate((start_sum, scatter_sum, gather_sum, share_sum)):
            pl.when(h == per - 1 + 2 * k)(functools.partial(stage, 0))

    patch = patch_ref[...]
    attention(
        qkv.at[:C], qkv.at[C : 2 * C], qkv.at[2 * C :], up,
        (patch == patch[:, :1]).astype(F),
        att, gqkv.at[:C], gqkv.at[C : 2 * C], gqkv.at[2 * C :], after,
    )
    start_sum(1)

    grad_normed = jnp.dot(w_qkv_ref[...], gqkv[...], preferred_element_type=F)
    scaled = grad_normed * gain
    d_norm = recip * (
        scaled
        - jnp.mean(scaled, axis=0, keepdims=True)
        - normed[...] * jnp.mean(scaled * normed[...], axis=0, keepdims=True)
    )
    d_rows = (d_mixed_ref[...].astype(F).T + d_norm).astype(B)
    come = (p == at).astype(F).astype(B)
    back = jnp.dot(d_rows, come, preferred_element_type=F)
    back = jnp.where(lane < CAP, back[:128], jnp.where(lane < 2 * CAP, back[128:], 0.0))
    send[...] = back.T.astype(B)
    exchange(send, ret_ref, back_sems.at[0], back_sems.at[1])
    scatter_sum(1)
    stay = (p == here).astype(F).astype(B)
    local_ref[...] = jnp.dot(d_rows, stay, preferred_element_type=F).astype(B)
    mixed_ref[...] = (hil[...].astype(F) + dg(att[...], w_out_ref[...], 0, 0)).astype(B)
    gather_sum(1)
    await_exchange(ret_ref, back_sems.at[1])
    await_exchange(send, back_sems.at[0])
    share_sum(1)
    end_sum(0)
    end_sum(1)


def finish_kernel(
    code_ref, ret_ref, local_ref, sums_ref, w_qkv_ref, gain_ref,
    d_feats_ref, g_qkv_ref, g_out_ref, g_gain_ref,
):
    t = iota((PEERS * ROWS, 128), 0) % ROWS
    chosen = slot_rows(code_ref[...]).astype(F).astype(B)
    d_feats = dg(halves(ret_ref[...], t), chosen, 0, 0) + local_ref[...].astype(F)
    d_feats_ref[...] = d_feats.T.astype(B)
    for side in range(2):
        lanes = slice(side * 128, (side + 1) * 128)
        column = jnp.zeros((128, 128), F)
        for g in range(GROUPS):
            for m in range(4):
                first = (2 * g + m // 2) * HALF + side * 2 * WIDE + (m % 2) * WIDE
                part = sums_ref[first : first + WIDE, :].astype(F)
                if m < 3:
                    at = slice(m * C + g * WIDE, m * C + (g + 1) * WIDE)
                    part = part.T
                    g_qkv_ref[lanes, at] = part
                    column += part * w_qkv_ref[lanes, at].astype(F)
                else:
                    g_out_ref[g * WIDE : (g + 1) * WIDE, lanes] = part
        total_row = jnp.sum(column.T, axis=0, keepdims=True)
        g_gain_ref[:, lanes] = total_row / gain_ref[:, lanes]


def call(kernel, out_shapes, n_in, scratch=(), collective_id=None):
    params = dict(vmem_limit_bytes=VMEM)
    if collective_id is not None:
        params.update(collective_id=collective_id, has_side_effects=True)
    return pl.pallas_call(
        kernel,
        out_shape=[jax.ShapeDtypeStruct(s, d) for s, d in out_shapes],
        in_specs=[ANYWHERE] * n_in,
        out_specs=[ANYWHERE] * len(out_shapes),
        scratch_shapes=list(scratch),
        compiler_params=pltpu.CompilerParams(**params),
    )


def on_device(feats, hilbert_rank, patch_id, gain, w_qkv, w_out, d_mixed):
    rank = hilbert_rank.reshape(1, N)
    patch = patch_id.reshape(1, N)
    gain = gain.reshape(1, C)
    blocks = (PEERS * ROWS, 128)
    sums_shape = (GROUPS * 2 * HALF, 128)
    dma = pltpu.SemaphoreType.DMA
    by_point, by_channel = (N, C), (C, N)
    code, mixed, local, ret, sums = call(
        layer_kernel,
        [((1, N), I), (by_point, B), (by_channel, B), (blocks, B), (sums_shape, B)],
        7,
        [
            pltpu.VMEM(blocks, B), pltpu.VMEM(blocks, B), pltpu.VMEM(by_point, B),
            pltpu.VMEM((3 * C, N), B), pltpu.VMEM(by_channel, B), pltpu.VMEM(by_channel, F),
            pltpu.VMEM(by_channel, B), pltpu.VMEM(by_point, B), pltpu.VMEM(by_channel, B),
            pltpu.VMEM((3 * C, N), B), pltpu.VMEM((2 * HALF, 128), F),
        ]
        + [pltpu.VMEM((GROUPS, HALF, 128), B)] * 5
        + [dma((2,))] * 2
        + [dma((GROUPS, 2))] * 4,
        collective_id=0,
    )(rank, feats, patch, gain, w_qkv, w_out, d_mixed)
    d_feats, g_qkv, g_out, g_gain = call(
        finish_kernel, [((N, C), B), ((C, 3 * C), F), ((C, C), F), ((1, C), F)], 6
    )(code, ret, local, sums, w_qkv, gain)
    return (mixed, d_feats, g_qkv, g_out, g_gain.reshape(C))


def solution(mesh):
    return jax.shard_map(
        on_device,
        mesh=mesh,
        in_specs=(
            P(("rep", "seq"), None),
            P(("rep", "seq")),
            P(("rep", "seq")),
            P(),
            P(),
            P(),
            P(("rep", "seq"), None),
        ),
        out_specs=(
            P(("rep", "seq"), None),
            P(("rep", "seq"), None),
            P("rep", None),
            P("rep", None),
            P("rep"),
        ),
        check_vma=False,
    )
```

```python
import functools

import jax
import jax.numpy as jnp
from jax import lax
from jax.experimental import pallas as pl
from jax.experimental.pallas import tpu as pltpu
from jax.sharding import PartitionSpec as P

F = jnp.float32
B = jnp.bfloat16
I = jnp.int32

N = 1024
C = 256
HDIM = 16
HEADS = C // HDIM
PEERS = 64
CAP = 4
SLOTS = PEERS * CAP
CHIPS = 32
WIDE = C // 2
PIECE = 16
HALF = CHIPS * PIECE
PAIR = 2 * HDIM
OWNERS = 16
PAIRS = 4
EPS = 1e-05
MASKED = 1e30
LOG2E = 1.4426950408889634
UNROLL = 2
VMEM = 56 << 20

ANYWHERE = pl.BlockSpec(memory_space=pltpu.VMEM)


def dg(a, b, ca, cb):
    return lax.dot_general(a, b, (((ca,), (cb,)), ((), ())), preferred_element_type=F)


def iota(shape, dim):
    return lax.broadcasted_iota(I, shape, dim)


def greet():
    me = lax.axis_index("seq")
    barrier = pltpu.get_barrier_semaphore()

    def signal(step, carry):
        peer = lax.rem(me + step, PEERS)
        pl.semaphore_signal(
            barrier, inc=1, device_id={"seq": peer}, device_id_type=pl.DeviceIdType.MESH
        )
        return carry

    lax.fori_loop(1, PEERS, signal, 0)


def met():
    pl.semaphore_wait(pltpu.get_barrier_semaphore(), PEERS - 1)


def remote(src, dst, send_sem, recv_sem, peer):
    return pltpu.make_async_remote_copy(
        src_ref=src,
        dst_ref=dst,
        send_sem=send_sem,
        recv_sem=recv_sem,
        device_id={"seq": peer},
        device_id_type=pl.DeviceIdType.MESH,
    )


def await_bytes(ref, sem):
    pltpu.make_async_copy(ref, ref, sem).wait()


def exchange(src, dst, send_sem, recv_sem):
    me = lax.axis_index("seq")

    def send(step, carry):
        peer = lax.rem(me + step, PEERS)
        remote(src.at[peer], dst.at[me], send_sem, recv_sem, peer).start()
        return carry

    lax.fori_loop(1, PEERS, send, 0)


def await_exchange(ref, sem):
    await_bytes(ref.at[pl.ds(0, PEERS - 1)], sem)


def slot_rows(code):
    return (iota((SLOTS, 1), 0) == code).astype(F).astype(B)


def split(x):
    high = x.astype(B)
    return high, (x - high.astype(F)).astype(B)


def attention(q_ref, k_ref, v_ref, u_ref, group, att, gq, gk, gv, after):
    one = jnp.where(group > 0, 1.0, 0.0)
    pad = jnp.zeros((HDIM - 2, N), F)
    q_bias = jnp.concatenate([-MASKED * (1 - one), -MASKED * one, pad], 0).astype(B)
    k_bias = jnp.concatenate([one, 1 - one, pad], 0).astype(B)
    ones = jnp.concatenate([jnp.ones((1, N), F), jnp.zeros((HDIM - 1, N), F)], 0).astype(B)
    scale = HDIM ** (-0.5)

    def head(h):
        rows = pl.ds(pl.multiple_of(h * HDIM, HDIM), HDIM)
        q, k, v = q_ref[rows, :], k_ref[rows, :], v_ref[rows, :]
        q_wide, k_wide, v_wide = q.astype(F), k.astype(F), v.astype(F)
        u = u_ref[rows, :].astype(F)
        center = jnp.mean(v_wide, axis=1, keepdims=True)
        v_wide = v_wide - center
        q_high, q_low = split(q_wide * (scale * LOG2E))
        scores = dg(
            jnp.concatenate([k, k, k_bias], 0), jnp.concatenate([q_high, q_low, q_bias], 0), 0, 0
        )
        low = jnp.exp2(scores - jnp.max(scores, axis=0, keepdims=True)).astype(B)
        left = [v, ones, k] + [(v_wide[a : a + 1] * k_wide).astype(B) for a in range(HDIM)]
        sums = jnp.dot(jnp.concatenate(left, 0), low, preferred_element_type=F)
        recip = 1.0 / sums[HDIM : HDIM + 1]
        attended = sums[:HDIM] * recip
        delta = jnp.sum(u * (attended - center), axis=0, keepdims=True)
        grad = -delta * sums[2 * HDIM : 3 * HDIM]
        for a in range(HDIM):
            grad += u[a : a + 1] * sums[(3 + a) * HDIM : (4 + a) * HDIM]
        att[rows, :] = attended.astype(B)
        gq[rows, :] = (grad * (recip * scale)).astype(B)
        u = u * recip
        q_wide = q_wide * scale
        left = [u.astype(B), (q_wide * (-delta * recip)).astype(B)]
        left += [(u[a : a + 1] * q_wide).astype(B) for a in range(HDIM)]
        sums = dg(jnp.concatenate(left, 0), low, 1, 1)
        grad = sums[HDIM : 2 * HDIM]
        for a in range(HDIM):
            grad += v_wide[a : a + 1] * sums[(2 + a) * HDIM : (3 + a) * HDIM]
        gv[rows, :] = sums[:HDIM].astype(B)
        gk[rows, :] = grad.astype(B)

    def heads(i, carry):
        for j in range(UNROLL):
            head(i * UNROLL + j)
        after(i * UNROLL + UNROLL - 1)
        return carry

    lax.fori_loop(0, HEADS // UNROLL, heads, 0)


def layer_kernel(
    rank_ref, feats_ref, patch_ref, gain_ref, w_qkv_ref, w_out_ref, d_mixed_ref,
    code_ref, mixed_ref, local_ref, ret_ref, sums_ref, tails_ref,
    send, got, flat, back_send, back_got,
    hil, qkv, up, normed, low, low_rows, att, gqkv, chunk,
    half_send, half_got, piece_send, piece_got, done, pair_send, pair_got,
    go_sems, back_sems, half_sems, piece_sems, done_sems, last_sems, pair_sems, tail_sems,
):
    greet()
    me = lax.axis_index("seq")
    core = lax.rem(me, 2)
    chip = me // 2
    partner = chip * 2 + 1 - core
    own = pl.ds(pl.multiple_of(chip * PIECE, PIECE), PIECE)
    mine = pl.ds(pl.multiple_of(me * PIECE, PIECE), PIECE)
    others = pl.ds(0, (CHIPS - 1) * PIECE)
    peers = pl.ds(0, (PEERS - 1) * PIECE)

    rank = rank_ref[...]
    owner = rank // N
    onehot = (iota((PEERS, N), 0) == owner).astype(F)
    upto = (iota((N, N), 0) <= iota((N, N), 1)).astype(F).astype(B)
    count = jnp.dot(onehot.astype(B), upto, preferred_element_type=F)
    slot = jnp.sum(count * onehot, axis=0, keepdims=True).astype(I) - 1
    code = jnp.where(owner == me, -1, owner * CAP + slot)
    code_ref[...] = code
    chosen = slot_rows(code)
    spot = rank % N
    k = iota((128, N), 0)
    extra = jnp.where(k == 0, spot // 32, jnp.where(k == 1, spot % 32, jnp.where(k == 2, 1, 0)))
    rows = jnp.dot(chosen, feats_ref[...], preferred_element_type=F)
    spots = dg(chosen, extra.astype(F).astype(B), 1, 1)
    for o in range(PEERS):
        send[o, :, :C] = rows[o * CAP : (o + 1) * CAP].astype(B)
        send[o, :, C:] = spots[o * CAP : (o + 1) * CAP].astype(B)
    got[me] = jnp.zeros((CAP, C + 128), B)
    back_got[me] = jnp.zeros((CAP, C), B)
    met()
    exchange(send, got, go_sems.at[0], go_sems.at[1])

    here = jnp.where(owner == me, spot, -1)
    p = iota((N, 1), 0)
    stay = (p == here).astype(F).astype(B)
    hil[...] = jnp.dot(stay, feats_ref[...], preferred_element_type=F).astype(B)
    up[...] = dg(w_out_ref[...], d_mixed_ref[...], 1, 1).astype(B)
    gain = jnp.broadcast_to(gain_ref[...], (8, C)).T[:, :1]
    await_exchange(got, go_sems.at[1])
    await_exchange(send, go_sems.at[0])

    for o in range(PEERS):
        flat[o * CAP : (o + 1) * CAP, :] = got[o].astype(F)
    spots = flat[:, C:].astype(B)
    weight = iota((16, 128), 1)
    weight = jnp.where(weight == 0, 32.0, jnp.where(weight < 2, 1.0, 0.0)).astype(B)
    valid = jnp.where(iota((16, 128), 1) == 2, 1.0, 0.0).astype(B)
    at = dg(weight, spots, 1, 1)[:1]
    at = jnp.where(dg(valid, spots, 1, 1)[:1] > 0.5, at, -1.0).astype(I)
    come = (p == at).astype(F).astype(B)
    rows = hil[...].astype(F)
    rows += jnp.dot(come, flat[:, :C].astype(B), preferred_element_type=F)
    hil[...] = rows.astype(B)

    wide = rows.T
    centred = wide - jnp.mean(wide, axis=0, keepdims=True)
    recip = lax.rsqrt(jnp.mean(centred * centred, axis=0, keepdims=True) + EPS)
    normed[...] = centred * recip
    scaled = normed[...] * gain
    low[...] = scaled.astype(B)
    low_rows[...] = scaled.T.astype(B)
    qkv[...] = dg(w_qkv_ref[...], low[...], 0, 0).astype(B)

    def gradients(first, wide):
        parts = [gqkv[pl.ds(m * C + first, wide), :] for m in range(3)]
        sums = [jnp.dot(part, low_rows[...], preferred_element_type=F) for part in parts]
        span = pl.ds(first, wide)
        return sums + [jnp.dot(att[span, :], d_mixed_ref[...], preferred_element_type=F)]

    def start_sum():
        sums = gradients(0, WIDE)
        for m in range(4):
            for side in range(2):
                first = (m // 2) * HALF + side * 2 * WIDE + (m % 2) * WIDE
                chunk[first : first + WIDE, :] = sums[m][:, side * 128 : (side + 1) * 128]
        theirs = pl.ds(pl.multiple_of((1 - core) * HALF, HALF), HALF)
        half_send[...] = chunk[theirs, :].astype(B)
        remote(half_send, half_got, half_sems.at[0], half_sems.at[1], partner).start()

    def scatter_sum():
        await_bytes(half_got, half_sems.at[1])
        kept = chunk[pl.ds(pl.multiple_of(core * HALF, HALF), HALF), :]
        piece_send[...] = (kept + half_got[...].astype(F)).astype(B)
        piece_got[own, :] = piece_send[own, :]

        def scatter(step, carry):
            to = lax.rem(chip + step, CHIPS)
            theirs = pl.ds(pl.multiple_of(to * PIECE, PIECE), PIECE)
            remote(
                piece_send.at[theirs], piece_got.at[own],
                piece_sems.at[0], piece_sems.at[1], to * 2 + core,
            ).start()
            return carry

        lax.fori_loop(1, CHIPS, scatter, 0)

    def total_of(pieces, count):
        total = pieces[0:PIECE, :].astype(F)
        for j in range(1, count):
            total += pieces[j * PIECE : (j + 1) * PIECE, :].astype(F)
        return total.astype(B)

    def gather_sum():
        await_bytes(piece_got.at[others], piece_sems.at[1])
        done[own, :] = total_of(piece_got, CHIPS)

        def gather(step, carry):
            to = lax.rem(chip + step, CHIPS)
            remote(
                done.at[own], done.at[own], done_sems.at[0], done_sems.at[1], to * 2 + core
            ).start()
            return carry

        lax.fori_loop(1, CHIPS, gather, 0)

    def share_sum():
        await_bytes(done.at[others], done_sems.at[1])
        kept = pl.ds(pl.multiple_of(core * HALF, HALF), HALF)
        remote(done, sums_ref.at[kept], last_sems.at[0], last_sems.at[1], partner).start()
        sums_ref[kept, :] = done[...]

    def end_sum():
        await_bytes(done, last_sems.at[1])
        await_bytes(done, last_sems.at[0])
        await_bytes(half_send, half_sems.at[0])
        await_bytes(piece_send.at[others], piece_sems.at[0])
        await_bytes(done.at[others], done_sems.at[0])

    turn = lax.rem(me, PAIRS)

    def start_pair(c):
        sums = gradients(pl.multiple_of(WIDE + c * PAIR, PAIR), PAIR)
        for m in range(4):
            for side in range(2):
                first = (side * 4 + m) * PAIR
                pair_send[c, first : first + PAIR, :] = sums[m][
                    :, side * 128 : (side + 1) * 128
                ].astype(B)

        def piece(m):
            return pair_send.at[c, pl.ds(pl.multiple_of(m * PIECE, PIECE), PIECE)]

        def scatter(step, carry):
            m = lax.rem(me // PAIRS + step, OWNERS)
            remote(
                piece(m), pair_got.at[mine], pair_sems.at[0], pair_sems.at[1], m * PAIRS + c
            ).start()
            return carry

        @pl.when(turn == c)
        def _():
            pair_got[mine, :] = piece(me // PAIRS)[...]

        @pl.when(turn != c)
        def _():
            scatter(0, 0)

        lax.fori_loop(1, OWNERS, scatter, 0)

    def finish_pair():
        await_bytes(pair_got.at[peers], pair_sems.at[1])
        tails_ref[mine, :] = total_of(pair_got, PEERS)

        def gather(step, carry):
            peer = lax.rem(me + step, PEERS)
            remote(
                tails_ref.at[mine], tails_ref.at[mine], tail_sems.at[0], tail_sems.at[1], peer
            ).start()
            return carry

        lax.fori_loop(1, PEERS, gather, 0)

    def after(h):
        for k, stage in enumerate((start_sum, scatter_sum, gather_sum, share_sum)):
            pl.when(h == HEADS // 2 - 1 + 2 * k)(stage)
        first = HEADS // 2 + 1
        for c in range(2):
            pl.when((h == first + 2 * c + 4) & (turn == c))(finish_pair)
        pl.when(h >= first)(lambda: start_pair((h - first) // 2))

    patch = patch_ref[...]
    attention(
        qkv.at[:C], qkv.at[C : 2 * C], qkv.at[2 * C :], up,
        (patch == patch[:, :1]).astype(F),
        att, gqkv.at[:C], gqkv.at[C : 2 * C], gqkv.at[2 * C :], after,
    )

    grad_normed = jnp.dot(w_qkv_ref[...], gqkv[...], preferred_element_type=F)
    scaled = grad_normed * gain
    d_norm = recip * (
        scaled
        - jnp.mean(scaled, axis=0, keepdims=True)
        - normed[...] * jnp.mean(scaled * normed[...], axis=0, keepdims=True)
    )
    d_rows = (d_mixed_ref[...].astype(F).T + d_norm).astype(B)
    come = (p == at).astype(F).astype(B)
    back = jnp.dot(d_rows, come, preferred_element_type=F).T
    for o in range(PEERS):
        back_send[o] = back[o * CAP : (o + 1) * CAP].astype(B)
    exchange(back_send, back_got, back_sems.at[0], back_sems.at[1])
    pl.when(turn >= 2)(finish_pair)
    stay = (p == here).astype(F).astype(B)
    local_ref[...] = jnp.dot(d_rows, stay, preferred_element_type=F).astype(B)
    mixed_ref[...] = (hil[...].astype(F) + dg(att[...], w_out_ref[...], 0, 0)).astype(B)
    end_sum()
    await_exchange(back_got, back_sems.at[1])
    await_exchange(back_send, back_sems.at[0])
    for o in range(PEERS):
        ret_ref[o * CAP : (o + 1) * CAP, :] = back_got[o]
    await_bytes(pair_got.at[peers], pair_sems.at[0])
    await_bytes(tails_ref.at[peers], tail_sems.at[1])
    await_bytes(tails_ref.at[peers], tail_sems.at[0])


def finish_kernel(
    code_ref, ret_ref, local_ref, sums_ref, tails_ref, w_qkv_ref, gain_ref,
    d_feats_ref, g_qkv_ref, g_out_ref, g_gain_ref,
):
    d_feats = dg(ret_ref[...], slot_rows(code_ref[...]), 0, 0) + local_ref[...].astype(F)
    d_feats_ref[...] = d_feats.T.astype(B)

    def sums(m, side):
        first = (m // 2) * HALF + side * 2 * WIDE + (m % 2) * WIDE
        yield sums_ref[first : first + WIDE, :].astype(F)
        tails = []
        for c in range(PAIRS):
            for part in range(2):
                first = (((side * 4 + m) * 2 + part) * PAIRS + c) * PIECE
                tails.append(tails_ref[first : first + PIECE, :].astype(F))
        yield jnp.concatenate(tails, 0)

    for side in range(2):
        lanes = slice(side * 128, (side + 1) * 128)
        column = jnp.zeros((128, 128), F)
        for m in range(4):
            for g, part in enumerate(sums(m, side)):
                if m < 3:
                    at = slice(m * C + g * WIDE, m * C + (g + 1) * WIDE)
                    part = part.T
                    g_qkv_ref[lanes, at] = part
                    column += part * w_qkv_ref[lanes, at].astype(F)
                else:
                    g_out_ref[g * WIDE : (g + 1) * WIDE, lanes] = part
        total_row = jnp.sum(column.T, axis=0, keepdims=True)
        g_gain_ref[:, lanes] = total_row / gain_ref[:, lanes]


def call(kernel, out_shapes, n_in, scratch=(), collective_id=None):
    params = dict(vmem_limit_bytes=VMEM)
    if collective_id is not None:
        params.update(collective_id=collective_id, has_side_effects=True)
    return pl.pallas_call(
        kernel,
        out_shape=[jax.ShapeDtypeStruct(s, d) for s, d in out_shapes],
        in_specs=[ANYWHERE] * n_in,
        out_specs=[ANYWHERE] * len(out_shapes),
        scratch_shapes=list(scratch),
        compiler_params=pltpu.CompilerParams(**params),
    )


def on_device(feats, hilbert_rank, patch_id, gain, w_qkv, w_out, d_mixed):
    rank = hilbert_rank.reshape(1, N)
    patch = patch_id.reshape(1, N)
    gain = gain.reshape(1, C)
    dma = pltpu.SemaphoreType.DMA
    by_point, by_channel = (N, C), (C, N)
    half, whole = (HALF, 128), (2 * HALF, 128)
    out_block, back_block = (PEERS, CAP, C + 128), (PEERS, CAP, C)
    code, mixed, local, ret, sums, tails = call(
        layer_kernel,
        [((1, N), I), (by_point, B), (by_channel, B), ((SLOTS, C), B), (whole, B), (whole, B)],
        7,
        [
            pltpu.VMEM(out_block, B), pltpu.VMEM(out_block, B), pltpu.VMEM((SLOTS, C + 128), F),
            pltpu.VMEM(back_block, B), pltpu.VMEM(back_block, B), pltpu.VMEM(by_point, B),
            pltpu.VMEM((3 * C, N), B), pltpu.VMEM(by_channel, B), pltpu.VMEM(by_channel, F),
            pltpu.VMEM(by_channel, B), pltpu.VMEM(by_point, B), pltpu.VMEM(by_channel, B),
            pltpu.VMEM((3 * C, N), B), pltpu.VMEM(whole, F),
        ]
        + [pltpu.VMEM(half, B)] * 5
        + [pltpu.VMEM((PAIRS, OWNERS * PIECE, 128), B), pltpu.VMEM(whole, B)]
        + [dma((2,))] * 8,
        collective_id=0,
    )(rank, feats, patch, gain, w_qkv, w_out, d_mixed)
    d_feats, g_qkv, g_out, g_gain = call(
        finish_kernel, [((N, C), B), ((C, 3 * C), F), ((C, C), F), ((1, C), F)], 7
    )(code, ret, local, sums, tails, w_qkv, gain)
    return (mixed, d_feats, g_qkv, g_out, g_gain.reshape(C))


def solution(mesh):
    return jax.shard_map(
        on_device,
        mesh=mesh,
        in_specs=(
            P(("rep", "seq"), None),
            P(("rep", "seq")),
            P(("rep", "seq")),
            P(),
            P(),
            P(),
            P(("rep", "seq"), None),
        ),
        out_specs=(
            P(("rep", "seq"), None),
            P(("rep", "seq"), None),
            P("rep", None),
            P("rep", None),
            P("rep"),
        ),
        check_vma=False,
    )
```

```python
import functools

import jax
import jax.numpy as jnp
from jax import lax
from jax.experimental import pallas as pl
from jax.experimental.pallas import tpu as pltpu
from jax.sharding import PartitionSpec as P

F = jnp.float32
B = jnp.bfloat16
I = jnp.int32

N = 1024
C = 256
HDIM = 16
HEADS = C // HDIM
PEERS = 64
CAP = 4
SLOTS = PEERS * CAP
CHIPS = 32
WIDE = C // 2
PIECE = 16
HALF = CHIPS * PIECE
PAIR = 2 * HDIM
OWNERS = 16
PAIRS = 4
EPS = 1e-05
MASKED = 1e30
LOG2E = 1.4426950408889634
HALVES = 2
VMEM = 56 << 20

VECTOR = pl.BlockSpec(memory_space=pltpu.VMEM)


def dg(a, b, ca, cb):
    return lax.dot_general(a, b, (((ca,), (cb,)), ((), ())), preferred_element_type=F)


def iota(shape, dim):
    return lax.broadcasted_iota(I, shape, dim)


def greet():
    me = lax.axis_index("seq")
    barrier = pltpu.get_barrier_semaphore()

    def signal(step):
        peer = lax.rem(me + step, PEERS)
        pl.semaphore_signal(
            barrier, inc=1, device_id={"seq": peer}, device_id_type=pl.DeviceIdType.MESH
        )

    for step in range(1, PEERS):
        signal(step)


def met():
    pl.semaphore_wait(pltpu.get_barrier_semaphore(), PEERS - 1)


def remote(src, dst, send_sem, recv_sem, peer):
    return pltpu.make_async_remote_copy(
        src_ref=src,
        dst_ref=dst,
        send_sem=send_sem,
        recv_sem=recv_sem,
        device_id={"seq": peer},
        device_id_type=pl.DeviceIdType.MESH,
    )


def await_bytes(ref, sem):
    pltpu.make_async_copy(ref, ref, sem).wait()


def exchange(src, dst, send_sem, recv_sem):
    me = lax.axis_index("seq")

    def send(step):
        peer = lax.rem(me + step, PEERS)
        remote(src.at[peer], dst.at[me], send_sem, recv_sem, peer).start()

    for step in range(1, PEERS):
        send(step)


def await_exchange(ref, sem):
    await_bytes(ref.at[pl.ds(0, PEERS - 1)], sem)


def slot_rows(code):
    return (iota((SLOTS, 1), 0) == code).astype(F).astype(B)


def split(x):
    high = x.astype(B)
    return high, (x - high.astype(F)).astype(B)


def attention(q_ref, k_ref, v_ref, u_ref, group, att, gq, gk, gv, expo, after):
    one = jnp.where(group > 0, 1.0, 0.0)
    pad = jnp.zeros((HDIM - 2, N), F)
    q_bias = jnp.concatenate([-MASKED * (1 - one), -MASKED * one, pad], 0).astype(B)
    k_bias = jnp.concatenate([one, 1 - one, pad], 0).astype(B)
    ones = jnp.concatenate([jnp.ones((1, N), F), jnp.zeros((HDIM - 1, N), F)], 0).astype(B)
    scale = HDIM ** (-0.5)

    def rows_of(h):
        return pl.ds(pl.multiple_of(h * HDIM, HDIM), HDIM)

    def softmax_of(h, slot):
        rows = rows_of(h)
        q_high, q_low = split(q_ref[rows, :].astype(F) * (scale * LOG2E))
        query = jnp.concatenate([q_high, q_low, q_bias], 0)
        k = k_ref[rows, :]
        keys = jnp.concatenate([k, k, k_bias], 0).astype(F).T.astype(B)
        wide = N // (2 * HALVES)

        def block(b):
            span = slice(b * wide, (b + 1) * wide)
            scores = jnp.dot(keys, query[:, span], preferred_element_type=F)
            top = jnp.max(scores, axis=0, keepdims=True)
            expo[slot, :, span] = jnp.exp2(scores - top).astype(B)

        return block

    def head(h, slot, beside):
        rows = rows_of(h)
        k, v = k_ref[rows, :], v_ref[rows, :]
        q_wide, k_wide, v_wide = q_ref[rows, :].astype(F) * scale, k.astype(F), v.astype(F)
        u_wide = u_ref[rows, :].astype(F)
        center = jnp.mean(v_wide, axis=1, keepdims=True)
        v_wide = v_wide - center
        left = [v, ones, k] + [(v_wide[a : a + 1] * k_wide).astype(B) for a in range(HDIM)]
        left = jnp.concatenate(left, 0)
        wide = N // HALVES
        spans = [slice(b * wide, (b + 1) * wide) for b in range(HALVES)]
        right = []
        for b, span in enumerate(spans):
            beside(b)
            sums = jnp.dot(left, expo[slot, :, span], preferred_element_type=F)
            recip = 1.0 / sums[HDIM : HDIM + 1]
            attended = sums[:HDIM] * recip
            u = u_wide[:, span]
            delta = jnp.sum(u * (attended - center), axis=0, keepdims=True)
            grad = -delta * sums[2 * HDIM : 3 * HDIM]
            for a in range(HDIM):
                grad += u[a : a + 1] * sums[(3 + a) * HDIM : (4 + a) * HDIM]
            att[rows, span] = attended.astype(B)
            gq[rows, span] = (grad * (recip * scale)).astype(B)
            u = u * recip
            q = q_wide[:, span]
            parts = [u.astype(B), (q * (-delta * recip)).astype(B)]
            parts += [(u[a : a + 1] * q).astype(B) for a in range(HDIM)]
            right.append(jnp.concatenate(parts, 0))
        right = jnp.concatenate(right, 1)
        for b, span in enumerate(spans):
            beside(HALVES + b)
            sums = dg(right, expo[slot, span, :], 1, 1)
            grad = sums[HDIM : 2 * HDIM]
            for a in range(HDIM):
                grad += v_wide[a : a + 1, span] * sums[(2 + a) * HDIM : (3 + a) * HDIM]
            gv[rows, span] = sums[:HDIM].astype(B)
            gk[rows, span] = grad.astype(B)

    first = softmax_of(0, 0)
    for b in range(2 * HALVES):
        first(b)

    def heads(i, carry):
        head(2 * i, 0, softmax_of(2 * i + 1, 1))
        head(2 * i + 1, 1, softmax_of(2 * i + 2, 0))
        after(2 * i + 1)
        return carry

    lax.fori_loop(0, HEADS // 2 - 1, heads, 0)
    head(HEADS - 2, 0, softmax_of(HEADS - 1, 1))
    head(HEADS - 1, 1, lambda b: None)


def layer_kernel(
    rank_ref, feats_ref, patch_ref, gain_ref, w_qkv_ref, w_out_ref, d_mixed_ref,
    code_ref, mixed_ref, local_ref, ret_ref, sums_ref, tails_ref,
    send, got, flat, back_send, back_got,
    hil, qkv, up, normed, low, low_rows, att, gqkv, chunk,
    half_send, half_got, piece_send, piece_got, done, pair_send, pair_got, expo,
    go_sems, back_sems, half_sems, piece_sems, done_sems, last_sems, pair_sems, tail_sems,
):
    greet()
    me = lax.axis_index("seq")
    core = lax.rem(me, 2)
    chip = me // 2
    partner = chip * 2 + 1 - core
    own = pl.ds(pl.multiple_of(chip * PIECE, PIECE), PIECE)
    mine = pl.ds(pl.multiple_of(me * PIECE, PIECE), PIECE)
    others = pl.ds(0, (CHIPS - 1) * PIECE)
    peers = pl.ds(0, (PEERS - 1) * PIECE)

    rank = rank_ref[...]
    owner = rank // N
    onehot = (iota((PEERS, N), 0) == owner).astype(F)
    upto = (iota((N, N), 0) <= iota((N, N), 1)).astype(F).astype(B)
    count = jnp.dot(onehot.astype(B), upto, preferred_element_type=F)
    slot = jnp.sum(count * onehot, axis=0, keepdims=True).astype(I) - 1
    code = jnp.where(owner == me, -1, owner * CAP + slot)
    code_ref[...] = code
    chosen = slot_rows(code)
    spot = rank % N
    k = iota((128, N), 0)
    extra = jnp.where(k == 0, spot // 32, jnp.where(k == 1, spot % 32, jnp.where(k == 2, 1, 0)))
    rows = jnp.dot(chosen, feats_ref[...], preferred_element_type=F)
    spots = dg(chosen, extra.astype(F).astype(B), 1, 1)
    for o in range(PEERS):
        send[o, :, :C] = rows[o * CAP : (o + 1) * CAP].astype(B)
        send[o, :, C:] = spots[o * CAP : (o + 1) * CAP].astype(B)
    got[me] = jnp.zeros((CAP, C + 128), B)
    back_got[me] = jnp.zeros((CAP, C), B)
    met()
    exchange(send, got, go_sems.at[0], go_sems.at[1])

    here = jnp.where(owner == me, spot, -1)
    p = iota((N, 1), 0)
    stay = (p == here).astype(F).astype(B)
    hil[...] = jnp.dot(stay, feats_ref[...], preferred_element_type=F).astype(B)
    up[...] = dg(w_out_ref[...], d_mixed_ref[...], 1, 1).astype(B)
    gain = jnp.broadcast_to(gain_ref[...], (8, C)).T[:, :1]
    await_exchange(got, go_sems.at[1])
    await_exchange(send, go_sems.at[0])

    for o in range(PEERS):
        flat[o * CAP : (o + 1) * CAP, :] = got[o].astype(F)
    spots = flat[:, C:].astype(B)
    weight = iota((16, 128), 1)
    weight = jnp.where(weight == 0, 32.0, jnp.where(weight < 2, 1.0, 0.0)).astype(B)
    valid = jnp.where(iota((16, 128), 1) == 2, 1.0, 0.0).astype(B)
    at = dg(weight, spots, 1, 1)[:1]
    at = jnp.where(dg(valid, spots, 1, 1)[:1] > 0.5, at, -1.0).astype(I)
    come = (p == at).astype(F).astype(B)
    rows = hil[...].astype(F)
    rows += jnp.dot(come, flat[:, :C].astype(B), preferred_element_type=F)
    hil[...] = rows.astype(B)

    wide = rows.T
    centred = wide - jnp.mean(wide, axis=0, keepdims=True)
    recip = lax.rsqrt(jnp.mean(centred * centred, axis=0, keepdims=True) + EPS)
    normed[...] = centred * recip
    scaled = normed[...] * gain
    low[...] = scaled.astype(B)
    low_rows[...] = scaled.T.astype(B)
    qkv[...] = dg(w_qkv_ref[...], low[...], 0, 0).astype(B)

    def gradients(first, wide):
        parts = [gqkv[pl.ds(m * C + first, wide), :] for m in range(3)]
        sums = jnp.dot(jnp.concatenate(parts, 0), low_rows[...], preferred_element_type=F)
        sums = [sums[m * wide : (m + 1) * wide] for m in range(3)]
        span = pl.ds(first, wide)
        return sums + [jnp.dot(att[span, :], d_mixed_ref[...], preferred_element_type=F)]

    def start_sum():
        sums = gradients(0, WIDE)
        for m in range(4):
            for side in range(2):
                first = (m // 2) * HALF + side * 2 * WIDE + (m % 2) * WIDE
                chunk[first : first + WIDE, :] = sums[m][:, side * 128 : (side + 1) * 128]
        theirs = pl.ds(pl.multiple_of((1 - core) * HALF, HALF), HALF)
        half_send[...] = chunk[theirs, :].astype(B)
        remote(half_send, half_got, half_sems.at[0], half_sems.at[1], partner).start()

    def scatter_sum():
        await_bytes(half_got, half_sems.at[1])
        kept = chunk[pl.ds(pl.multiple_of(core * HALF, HALF), HALF), :]
        piece_send[...] = (kept + half_got[...].astype(F)).astype(B)
        piece_got[own, :] = piece_send[own, :]

        def scatter(step):
            to = lax.rem(chip + step, CHIPS)
            theirs = pl.ds(pl.multiple_of(to * PIECE, PIECE), PIECE)
            remote(
                piece_send.at[theirs], piece_got.at[own],
                piece_sems.at[0], piece_sems.at[1], to * 2 + core,
            ).start()

        for step in range(1, CHIPS):
            scatter(step)

    def total_of(pieces, count):
        total = pieces[0:PIECE, :].astype(F)
        for j in range(1, count):
            total += pieces[j * PIECE : (j + 1) * PIECE, :].astype(F)
        return total.astype(B)

    def gather_sum():
        await_bytes(piece_got.at[others], piece_sems.at[1])
        done[own, :] = total_of(piece_got, CHIPS)

        def gather(step):
            to = lax.rem(chip + step, CHIPS)
            remote(
                done.at[own], done.at[own], done_sems.at[0], done_sems.at[1], to * 2 + core
            ).start()

        for step in range(1, CHIPS):
            gather(step)

    def share_sum():
        await_bytes(done.at[others], done_sems.at[1])
        kept = pl.ds(pl.multiple_of(core * HALF, HALF), HALF)
        remote(done, sums_ref.at[kept], last_sems.at[0], last_sems.at[1], partner).start()
        sums_ref[kept, :] = done[...]

    def end_sum():
        await_bytes(done, last_sems.at[1])
        await_bytes(done, last_sems.at[0])
        await_bytes(half_send, half_sems.at[0])
        await_bytes(piece_send.at[others], piece_sems.at[0])
        await_bytes(done.at[others], done_sems.at[0])

    turn = lax.rem(me, PAIRS)

    def start_pair(c):
        sums = gradients(WIDE + c * PAIR if isinstance(c, int) else pl.multiple_of(WIDE + c * PAIR, PAIR), PAIR)
        for m in range(4):
            for side in range(2):
                first = (side * 4 + m) * PAIR
                pair_send[c, first : first + PAIR, :] = sums[m][
                    :, side * 128 : (side + 1) * 128
                ].astype(B)

        def piece(m):
            return pair_send.at[c, pl.ds(pl.multiple_of(m * PIECE, PIECE), PIECE)]

        def scatter(step):
            m = lax.rem(me // PAIRS + step, OWNERS)
            remote(
                piece(m), pair_got.at[mine], pair_sems.at[0], pair_sems.at[1], m * PAIRS + c
            ).start()

        @pl.when(turn == c)
        def _():
            pair_got[mine, :] = piece(me // PAIRS)[...]

        @pl.when(turn != c)
        def _():
            scatter(0)

        for step in range(1, OWNERS):
            scatter(step)

    def finish_pair():
        await_bytes(pair_got.at[peers], pair_sems.at[1])
        tails_ref[mine, :] = total_of(pair_got, PEERS)

        def gather(step):
            peer = lax.rem(me + step, PEERS)
            remote(
                tails_ref.at[mine], tails_ref.at[mine], tail_sems.at[0], tail_sems.at[1], peer
            ).start()

        for step in range(1, PEERS):
            gather(step)

    def after(h):
        for k, stage in enumerate((start_sum, scatter_sum, gather_sum, share_sum)):
            pl.when(h == HEADS // 2 - 1 + 2 * k)(stage)
        first = HEADS // 2 + 1
        pl.when(h >= first)(lambda: start_pair((h - first) // 2))

    patch = patch_ref[...]
    attention(
        qkv.at[:C], qkv.at[C : 2 * C], qkv.at[2 * C :], up,
        (patch == patch[:, :1]).astype(F),
        att, gqkv.at[:C], gqkv.at[C : 2 * C], gqkv.at[2 * C :], expo, after,
    )

    start_pair(PAIRS - 1)

    grad_normed = jnp.dot(w_qkv_ref[...], gqkv[...], preferred_element_type=F)
    scaled = grad_normed * gain
    d_norm = recip * (
        scaled
        - jnp.mean(scaled, axis=0, keepdims=True)
        - normed[...] * jnp.mean(scaled * normed[...], axis=0, keepdims=True)
    )
    d_rows = (d_mixed_ref[...].astype(F).T + d_norm).astype(B)
    come = (p == at).astype(F).astype(B)
    back = jnp.dot(d_rows, come, preferred_element_type=F).T
    for o in range(PEERS):
        back_send[o] = back[o * CAP : (o + 1) * CAP].astype(B)
    exchange(back_send, back_got, back_sems.at[0], back_sems.at[1])
    finish_pair()
    stay = (p == here).astype(F).astype(B)
    local_ref[...] = jnp.dot(d_rows, stay, preferred_element_type=F).astype(B)
    mixed_ref[...] = (hil[...].astype(F) + dg(att[...], w_out_ref[...], 0, 0)).astype(B)
    end_sum()
    await_exchange(back_got, back_sems.at[1])
    await_exchange(back_send, back_sems.at[0])
    for o in range(PEERS):
        ret_ref[o * CAP : (o + 1) * CAP, :] = back_got[o]
    await_bytes(pair_got.at[peers], pair_sems.at[0])
    await_bytes(tails_ref.at[peers], tail_sems.at[1])
    await_bytes(tails_ref.at[peers], tail_sems.at[0])


def finish_kernel(
    code_ref, ret_ref, local_ref, sums_ref, tails_ref, w_qkv_ref, gain_ref, rows_ref,
    d_feats_ref, g_qkv_ref, g_out_ref, g_gain_ref, mixed_ref, sem,
):
    copy = pltpu.make_async_copy(rows_ref, mixed_ref, sem)
    copy.start()
    d_feats = dg(ret_ref[...], slot_rows(code_ref[...]), 0, 0) + local_ref[...].astype(F)
    d_feats_ref[...] = d_feats.T.astype(B)

    def sums(m, side):
        first = (m // 2) * HALF + side * 2 * WIDE + (m % 2) * WIDE
        yield sums_ref[first : first + WIDE, :].astype(F)
        tails = []
        for c in range(PAIRS):
            for part in range(2):
                first = (((side * 4 + m) * 2 + part) * PAIRS + c) * PIECE
                tails.append(tails_ref[first : first + PIECE, :].astype(F))
        yield jnp.concatenate(tails, 0)

    for side in range(2):
        lanes = slice(side * 128, (side + 1) * 128)
        column = jnp.zeros((128, 128), F)
        for m in range(4):
            for g, part in enumerate(sums(m, side)):
                if m < 3:
                    at = slice(m * C + g * WIDE, m * C + (g + 1) * WIDE)
                    part = part.T
                    g_qkv_ref[lanes, at] = part
                    column += part * w_qkv_ref[lanes, at].astype(F)
                else:
                    g_out_ref[g * WIDE : (g + 1) * WIDE, lanes] = part
        total_row = jnp.sum(column.T, axis=0, keepdims=True)
        g_gain_ref[:, lanes] = total_row / gain_ref[:, lanes]
    copy.wait()


def call(kernel, out_shapes, n_in, scratch=(), collective_id=None, through=0):
    params = dict(vmem_limit_bytes=VMEM)
    if collective_id is not None:
        params.update(collective_id=collective_id, has_side_effects=True)
    return pl.pallas_call(
        kernel,
        out_shape=[jax.ShapeDtypeStruct(s, d) for s, d in out_shapes],
        in_specs=[VECTOR] * (n_in - through) + [pl.BlockSpec(memory_space=pl.ANY)] * through,
        out_specs=[VECTOR] * (len(out_shapes) - through)
        + [pl.BlockSpec(memory_space=pl.ANY)] * through,
        scratch_shapes=list(scratch),
        compiler_params=pltpu.CompilerParams(**params),
    )


def on_device(feats, hilbert_rank, patch_id, gain, w_qkv, w_out, d_mixed):
    rank = hilbert_rank.reshape(1, N)
    patch = patch_id.reshape(1, N)
    gain = gain.reshape(1, C)
    dma = pltpu.SemaphoreType.DMA
    by_point, by_channel = (N, C), (C, N)
    half, whole = (HALF, 128), (2 * HALF, 128)
    out_block, back_block = (PEERS, CAP, C + 128), (PEERS, CAP, C)
    code, mixed, local, ret, sums, tails = call(
        layer_kernel,
        [((1, N), I), (by_point, B), (by_channel, B), ((SLOTS, C), B), (whole, B), (whole, B)],
        7,
        [
            pltpu.VMEM(out_block, B), pltpu.VMEM(out_block, B), pltpu.VMEM((SLOTS, C + 128), F),
            pltpu.VMEM(back_block, B), pltpu.VMEM(back_block, B), pltpu.VMEM(by_point, B),
            pltpu.VMEM((3 * C, N), B), pltpu.VMEM(by_channel, B), pltpu.VMEM(by_channel, F),
            pltpu.VMEM(by_channel, B), pltpu.VMEM(by_point, B), pltpu.VMEM(by_channel, B),
            pltpu.VMEM((3 * C, N), B), pltpu.VMEM(whole, F),
        ]
        + [pltpu.VMEM(half, B)] * 5
        + [pltpu.VMEM((PAIRS, OWNERS * PIECE, 128), B), pltpu.VMEM(whole, B)]
        + [pltpu.VMEM((2, N, N), B)]
        + [dma((2,))] * 8,
        collective_id=0,
    )(rank, feats, patch, gain, w_qkv, w_out, d_mixed)
    d_feats, g_qkv, g_out, g_gain, mixed = call(
        finish_kernel,
        [(by_point, B), ((C, 3 * C), F), ((C, C), F), ((1, C), F), (by_point, B)],
        8,
        [dma],
        through=1,
    )(code, ret, local, sums, tails, w_qkv, gain, mixed)
    return (mixed, d_feats, g_qkv, g_out, g_gain.reshape(C))


def solution(mesh):
    return jax.shard_map(
        on_device,
        mesh=mesh,
        in_specs=(
            P(("rep", "seq"), None),
            P(("rep", "seq")),
            P(("rep", "seq")),
            P(),
            P(),
            P(),
            P(("rep", "seq"), None),
        ),
        out_specs=(
            P(("rep", "seq"), None),
            P(("rep", "seq"), None),
            P("rep", None),
            P("rep", None),
            P("rep"),
        ),
        check_vma=False,
    )
```

```python
import functools

import jax
import jax.numpy as jnp
from jax import lax
from jax.experimental import pallas as pl
from jax.experimental.pallas import tpu as pltpu
from jax.sharding import PartitionSpec as P

F = jnp.float32
B = jnp.bfloat16
I = jnp.int32

N = 1024
C = 256
HDIM = 16
HEADS = C // HDIM
PEERS = 64
CAP = 4
SLOTS = PEERS * CAP
CHIPS = 32
WIDE = C // 2
PIECE = 16
HALF = CHIPS * PIECE
PAIR = 2 * HDIM
OWNERS = 16
PAIRS = 4
EPS = 1e-05
MASKED = 1e30
LOG2E = 1.4426950408889634
HALVES = 2
VMEM = 56 << 20

VECTOR = pl.BlockSpec(memory_space=pltpu.VMEM)


def dg(a, b, ca, cb):
    return lax.dot_general(a, b, (((ca,), (cb,)), ((), ())), preferred_element_type=F)


def iota(shape, dim):
    return lax.broadcasted_iota(I, shape, dim)


def greet():
    me = lax.axis_index("seq")
    barrier = pltpu.get_barrier_semaphore()

    def signal(step):
        peer = lax.rem(me + step, PEERS)
        pl.semaphore_signal(
            barrier, inc=1, device_id={"seq": peer}, device_id_type=pl.DeviceIdType.MESH
        )

    for step in range(1, PEERS):
        signal(step)


def met():
    pl.semaphore_wait(pltpu.get_barrier_semaphore(), PEERS - 1)


def remote(src, dst, send_sem, recv_sem, peer):
    return pltpu.make_async_remote_copy(
        src_ref=src,
        dst_ref=dst,
        send_sem=send_sem,
        recv_sem=recv_sem,
        device_id={"seq": peer},
        device_id_type=pl.DeviceIdType.MESH,
    )


def await_bytes(ref, sem):
    pltpu.make_async_copy(ref, ref, sem).wait()


def exchange(src, dst, send_sem, recv_sem):
    me = lax.axis_index("seq")

    def send(step):
        peer = lax.rem(me + step, PEERS)
        remote(src.at[peer], dst.at[me], send_sem, recv_sem, peer).start()

    for step in range(1, PEERS):
        send(step)


def await_exchange(ref, sem):
    await_bytes(ref.at[pl.ds(0, PEERS - 1)], sem)


def slot_rows(code):
    return (iota((SLOTS, 1), 0) == code).astype(F).astype(B)


def split(x):
    high = x.astype(B)
    return high, (x - high.astype(F)).astype(B)


def attention(q_ref, k_ref, v_ref, u_ref, group, att, gq, gk, gv, expo, after):
    one = jnp.where(group > 0, 1.0, 0.0)
    pad = jnp.zeros((HDIM - 2, N), F)
    q_bias = jnp.concatenate([-MASKED * (1 - one), -MASKED * one, pad], 0).astype(B)
    k_bias = jnp.concatenate([one, 1 - one, pad], 0).astype(B)
    ones = jnp.concatenate([jnp.ones((1, N), F), jnp.zeros((HDIM - 1, N), F)], 0).astype(B)
    scale = HDIM ** (-0.5)

    def rows_of(h):
        return pl.ds(pl.multiple_of(h * HDIM, HDIM), HDIM)

    def softmax_of(h, slot):
        rows = rows_of(h)
        q_high, q_low = split(q_ref[rows, :].astype(F) * (scale * LOG2E))
        query = jnp.concatenate([q_high, q_low, q_bias], 0)
        k = k_ref[rows, :]
        keys = jnp.concatenate([k, k, k_bias], 0).astype(F).T.astype(B)
        wide = N // (2 * HALVES)

        def block(b):
            span = slice(b * wide, (b + 1) * wide)
            scores = jnp.dot(keys, query[:, span], preferred_element_type=F)
            top = jnp.max(scores, axis=0, keepdims=True)
            expo[slot, :, span] = jnp.exp2(scores - top).astype(B)

        return block

    def head(h, slot, beside):
        rows = rows_of(h)
        k, v = k_ref[rows, :], v_ref[rows, :]
        q_wide, k_wide, v_wide = q_ref[rows, :].astype(F) * scale, k.astype(F), v.astype(F)
        u_wide = u_ref[rows, :].astype(F)
        center = jnp.mean(v_wide, axis=1, keepdims=True)
        v_wide = v_wide - center
        left = [v, ones, k] + [(v_wide[a : a + 1] * k_wide).astype(B) for a in range(HDIM)]
        left = jnp.concatenate(left, 0)
        wide = N // HALVES
        spans = [slice(b * wide, (b + 1) * wide) for b in range(HALVES)]
        right = []
        for b, span in enumerate(spans):
            beside(b)
            sums = jnp.dot(left, expo[slot, :, span], preferred_element_type=F)
            recip = 1.0 / sums[HDIM : HDIM + 1]
            attended = sums[:HDIM] * recip
            u = u_wide[:, span]
            delta = jnp.sum(u * (attended - center), axis=0, keepdims=True)
            grad = -delta * sums[2 * HDIM : 3 * HDIM]
            for a in range(HDIM):
                grad += u[a : a + 1] * sums[(3 + a) * HDIM : (4 + a) * HDIM]
            att[rows, span] = attended.astype(B)
            gq[rows, span] = (grad * (recip * scale)).astype(B)
            u = u * recip
            q = q_wide[:, span]
            parts = [u.astype(B), (q * (-delta * recip)).astype(B)]
            parts += [(u[a : a + 1] * q).astype(B) for a in range(HDIM)]
            right.append(jnp.concatenate(parts, 0))
        right = jnp.concatenate(right, 1)
        for b, span in enumerate(spans):
            beside(HALVES + b)
            sums = dg(right, expo[slot, span, :], 1, 1)
            grad = sums[HDIM : 2 * HDIM]
            for a in range(HDIM):
                grad += v_wide[a : a + 1, span] * sums[(2 + a) * HDIM : (3 + a) * HDIM]
            gv[rows, span] = sums[:HDIM].astype(B)
            gk[rows, span] = grad.astype(B)

    first = softmax_of(0, 0)
    for b in range(2 * HALVES):
        first(b)

    def heads(i, carry):
        head(2 * i, 0, softmax_of(2 * i + 1, 1))
        head(2 * i + 1, 1, softmax_of(2 * i + 2, 0))
        after(2 * i + 1)
        return carry

    lax.fori_loop(0, HEADS // 2 - 1, heads, 0)
    head(HEADS - 2, 0, softmax_of(HEADS - 1, 1))
    head(HEADS - 1, 1, lambda b: None)


def layer_kernel(
    rank_ref, feats_ref, patch_ref, gain_ref, w_qkv_ref, w_out_ref, d_mixed_ref,
    code_ref, mixed_ref, local_ref, ret_ref, sums_ref, tails_ref,
    send, got, flat, back_send, back_got,
    hil, qkv, up, normed, low, low_rows, att, gqkv, chunk,
    half_send, half_got, piece_send, piece_got, done, pair_send, pair_got, expo,
    go_sems, back_sems, half_sems, piece_sems, done_sems, last_sems, pair_sems, tail_sems,
):
    greet()
    me = lax.axis_index("seq")
    core = lax.rem(me, 2)
    chip = me // 2
    partner = chip * 2 + 1 - core
    own = pl.ds(pl.multiple_of(chip * PIECE, PIECE), PIECE)
    mine = pl.ds(pl.multiple_of(me * PIECE, PIECE), PIECE)
    others = pl.ds(0, (CHIPS - 1) * PIECE)
    peers = pl.ds(0, (PEERS - 1) * PIECE)

    rank = rank_ref[...]
    owner = rank // N
    onehot = (iota((PEERS, N), 0) == owner).astype(F)
    upto = (iota((N, N), 0) <= iota((N, N), 1)).astype(F).astype(B)
    count = jnp.dot(onehot.astype(B), upto, preferred_element_type=F)
    slot = jnp.sum(count * onehot, axis=0, keepdims=True).astype(I) - 1
    code = jnp.where(owner == me, -1, owner * CAP + slot)
    code_ref[...] = code
    chosen = slot_rows(code)
    spot = rank % N
    k = iota((128, N), 0)
    extra = jnp.where(k == 0, spot // 32, jnp.where(k == 1, spot % 32, jnp.where(k == 2, 1, 0)))
    rows = jnp.dot(chosen, feats_ref[...], preferred_element_type=F)
    spots = dg(chosen, extra.astype(F).astype(B), 1, 1)
    for o in range(PEERS):
        send[o, :, :C] = rows[o * CAP : (o + 1) * CAP].astype(B)
        send[o, :, C:] = spots[o * CAP : (o + 1) * CAP].astype(B)
    got[me] = jnp.zeros((CAP, C + 128), B)
    back_got[me] = jnp.zeros((CAP, C), B)
    met()
    exchange(send, got, go_sems.at[0], go_sems.at[1])

    here = jnp.where(owner == me, spot, -1)
    p = iota((N, 1), 0)
    stay = (p == here).astype(F).astype(B)
    hil[...] = jnp.dot(stay, feats_ref[...], preferred_element_type=F).astype(B)
    up[...] = dg(w_out_ref[...], d_mixed_ref[...], 1, 1).astype(B)
    gain = jnp.broadcast_to(gain_ref[...], (8, C)).T[:, :1]
    await_exchange(got, go_sems.at[1])
    await_exchange(send, go_sems.at[0])

    for o in range(PEERS):
        flat[o * CAP : (o + 1) * CAP, :] = got[o].astype(F)
    spots = flat[:, C:].astype(B)
    weight = iota((16, 128), 1)
    weight = jnp.where(weight == 0, 32.0, jnp.where(weight < 2, 1.0, 0.0)).astype(B)
    valid = jnp.where(iota((16, 128), 1) == 2, 1.0, 0.0).astype(B)
    at = dg(weight, spots, 1, 1)[:1]
    at = jnp.where(dg(valid, spots, 1, 1)[:1] > 0.5, at, -1.0).astype(I)
    come = (p == at).astype(F).astype(B)
    rows = hil[...].astype(F)
    rows += jnp.dot(come, flat[:, :C].astype(B), preferred_element_type=F)
    hil[...] = rows.astype(B)

    wide = rows.T
    centred = wide - jnp.mean(wide, axis=0, keepdims=True)
    recip = lax.rsqrt(jnp.mean(centred * centred, axis=0, keepdims=True) + EPS)
    normed[...] = centred * recip
    scaled = normed[...] * gain
    low[...] = scaled.astype(B)
    low_rows[...] = scaled.T.astype(B)
    qkv[...] = dg(w_qkv_ref[...], low[...], 0, 0).astype(B)

    def gradients(first, wide):
        parts = [gqkv[pl.ds(m * C + first, wide), :] for m in range(3)]
        sums = jnp.dot(jnp.concatenate(parts, 0), low_rows[...], preferred_element_type=F)
        sums = [sums[m * wide : (m + 1) * wide] for m in range(3)]
        span = pl.ds(first, wide)
        return sums + [jnp.dot(att[span, :], d_mixed_ref[...], preferred_element_type=F)]

    def start_sum():
        sums = gradients(0, WIDE)
        for m in range(4):
            for side in range(2):
                first = (m // 2) * HALF + side * 2 * WIDE + (m % 2) * WIDE
                chunk[first : first + WIDE, :] = sums[m][:, side * 128 : (side + 1) * 128]
        theirs = pl.ds(pl.multiple_of((1 - core) * HALF, HALF), HALF)
        half_send[...] = chunk[theirs, :].astype(B)
        remote(half_send, half_got, half_sems.at[0], half_sems.at[1], partner).start()

    def scatter_sum():
        await_bytes(half_got, half_sems.at[1])
        kept = chunk[pl.ds(pl.multiple_of(core * HALF, HALF), HALF), :]
        piece_send[...] = (kept + half_got[...].astype(F)).astype(B)
        piece_got[own, :] = piece_send[own, :]

        def scatter(step):
            to = lax.rem(chip + step, CHIPS)
            theirs = pl.ds(pl.multiple_of(to * PIECE, PIECE), PIECE)
            remote(
                piece_send.at[theirs], piece_got.at[own],
                piece_sems.at[0], piece_sems.at[1], to * 2 + core,
            ).start()

        for step in range(1, CHIPS):
            scatter(step)

    def total_of(pieces, count):
        total = pieces[0:PIECE, :].astype(F)
        for j in range(1, count):
            total += pieces[j * PIECE : (j + 1) * PIECE, :].astype(F)
        return total.astype(B)

    def gather_sum():
        await_bytes(piece_got.at[others], piece_sems.at[1])
        done[own, :] = total_of(piece_got, CHIPS)

        def gather(step):
            to = lax.rem(chip + step, CHIPS)
            remote(
                done.at[own], done.at[own], done_sems.at[0], done_sems.at[1], to * 2 + core
            ).start()

        for step in range(1, CHIPS):
            gather(step)

    def share_sum():
        await_bytes(done.at[others], done_sems.at[1])
        kept = pl.ds(pl.multiple_of(core * HALF, HALF), HALF)
        remote(done, sums_ref.at[kept], last_sems.at[0], last_sems.at[1], partner).start()
        sums_ref[kept, :] = done[...]

    def end_sum():
        await_bytes(done, last_sems.at[1])
        await_bytes(done, last_sems.at[0])
        await_bytes(half_send, half_sems.at[0])
        await_bytes(piece_send.at[others], piece_sems.at[0])
        await_bytes(done.at[others], done_sems.at[0])

    turn = lax.rem(me, PAIRS)

    def start_pair(c):
        sums = gradients(WIDE + c * PAIR if isinstance(c, int) else pl.multiple_of(WIDE + c * PAIR, PAIR), PAIR)
        for m in range(4):
            for side in range(2):
                first = (side * 4 + m) * PAIR
                pair_send[c, first : first + PAIR, :] = sums[m][
                    :, side * 128 : (side + 1) * 128
                ].astype(B)

        def piece(m):
            return pair_send.at[c, pl.ds(pl.multiple_of(m * PIECE, PIECE), PIECE)]

        def scatter(step):
            m = lax.rem(me // PAIRS + step, OWNERS)
            remote(
                piece(m), pair_got.at[mine], pair_sems.at[0], pair_sems.at[1], m * PAIRS + c
            ).start()

        @pl.when(turn == c)
        def _():
            pair_got[mine, :] = piece(me // PAIRS)[...]

        @pl.when(turn != c)
        def _():
            scatter(0)

        for step in range(1, OWNERS):
            scatter(step)

    def finish_pair():
        await_bytes(pair_got.at[peers], pair_sems.at[1])
        tails_ref[mine, :] = total_of(pair_got, PEERS)

        def gather(step):
            peer = lax.rem(me + step, PEERS)
            remote(
                tails_ref.at[mine], tails_ref.at[mine], tail_sems.at[0], tail_sems.at[1], peer
            ).start()

        for step in range(1, PEERS):
            gather(step)

    def after(h):
        for k, stage in enumerate((start_sum, scatter_sum, gather_sum, share_sum)):
            pl.when(h == HEADS // 2 - 1 + 2 * k)(stage)
        first = HEADS // 2 + 1
        pl.when(h >= first)(lambda: start_pair((h - first) // 2))

    patch = patch_ref[...]
    attention(
        qkv.at[:C], qkv.at[C : 2 * C], qkv.at[2 * C :], up,
        (patch == patch[:, :1]).astype(F),
        att, gqkv.at[:C], gqkv.at[C : 2 * C], gqkv.at[2 * C :], expo, after,
    )

    start_pair(PAIRS - 1)

    grad_normed = jnp.dot(w_qkv_ref[...], gqkv[...], preferred_element_type=F)
    scaled = grad_normed * gain
    d_norm = recip * (
        scaled
        - jnp.mean(scaled, axis=0, keepdims=True)
        - normed[...] * jnp.mean(scaled * normed[...], axis=0, keepdims=True)
    )
    d_rows = (d_mixed_ref[...].astype(F).T + d_norm).astype(B)
    come = (p == at).astype(F).astype(B)
    back = jnp.dot(d_rows, come, preferred_element_type=F).T
    for o in range(PEERS):
        back_send[o] = back[o * CAP : (o + 1) * CAP].astype(B)
    exchange(back_send, back_got, back_sems.at[0], back_sems.at[1])
    finish_pair()
    stay = (p == here).astype(F).astype(B)
    local_ref[...] = jnp.dot(d_rows, stay, preferred_element_type=F).astype(B)
    mixed_ref[...] = (hil[...].astype(F) + dg(att[...], w_out_ref[...], 0, 0)).astype(B)
    end_sum()
    await_exchange(back_got, back_sems.at[1])
    await_exchange(back_send, back_sems.at[0])
    for o in range(PEERS):
        ret_ref[o * CAP : (o + 1) * CAP, :] = back_got[o]
    await_bytes(pair_got.at[peers], pair_sems.at[0])
    await_bytes(tails_ref.at[peers], tail_sems.at[1])
    await_bytes(tails_ref.at[peers], tail_sems.at[0])


def finish_kernel(
    code_ref, ret_ref, local_ref, sums_ref, tails_ref, w_qkv_ref, gain_ref, rows_ref,
    d_feats_ref, g_qkv_ref, g_out_ref, g_gain_ref, mixed_ref,
):
    mixed_ref[...] = rows_ref[...]
    d_feats = dg(ret_ref[...], slot_rows(code_ref[...]), 0, 0) + local_ref[...].astype(F)
    d_feats_ref[...] = d_feats.T.astype(B)

    def sums(m, side):
        first = (m // 2) * HALF + side * 2 * WIDE + (m % 2) * WIDE
        yield sums_ref[first : first + WIDE, :].astype(F)
        tails = []
        for c in range(PAIRS):
            for part in range(2):
                first = (((side * 4 + m) * 2 + part) * PAIRS + c) * PIECE
                tails.append(tails_ref[first : first + PIECE, :].astype(F))
        yield jnp.concatenate(tails, 0)

    for side in range(2):
        lanes = slice(side * 128, (side + 1) * 128)
        column = jnp.zeros((128, 128), F)
        for m in range(4):
            for g, part in enumerate(sums(m, side)):
                if m < 3:
                    at = slice(m * C + g * WIDE, m * C + (g + 1) * WIDE)
                    part = part.T
                    g_qkv_ref[lanes, at] = part
                    column += part * w_qkv_ref[lanes, at].astype(F)
                else:
                    g_out_ref[g * WIDE : (g + 1) * WIDE, lanes] = part
        total_row = jnp.sum(column.T, axis=0, keepdims=True)
        g_gain_ref[:, lanes] = total_row / gain_ref[:, lanes]


def call(kernel, out_shapes, n_in, scratch=(), collective_id=None):
    params = dict(vmem_limit_bytes=VMEM)
    if collective_id is not None:
        params.update(collective_id=collective_id, has_side_effects=True)
    return pl.pallas_call(
        kernel,
        out_shape=[jax.ShapeDtypeStruct(s, d) for s, d in out_shapes],
        in_specs=[VECTOR] * n_in,
        out_specs=[VECTOR] * len(out_shapes),
        scratch_shapes=list(scratch),
        compiler_params=pltpu.CompilerParams(**params),
    )


def on_device(feats, hilbert_rank, patch_id, gain, w_qkv, w_out, d_mixed):
    rank = hilbert_rank.reshape(1, N)
    patch = patch_id.reshape(1, N)
    gain = gain.reshape(1, C)
    dma = pltpu.SemaphoreType.DMA
    by_point, by_channel = (N, C), (C, N)
    half, whole = (HALF, 128), (2 * HALF, 128)
    out_block, back_block = (PEERS, CAP, C + 128), (PEERS, CAP, C)
    code, mixed, local, ret, sums, tails = call(
        layer_kernel,
        [((1, N), I), (by_point, B), (by_channel, B), ((SLOTS, C), B), (whole, B), (whole, B)],
        7,
        [
            pltpu.VMEM(out_block, B), pltpu.VMEM(out_block, B), pltpu.VMEM((SLOTS, C + 128), F),
            pltpu.VMEM(back_block, B), pltpu.VMEM(back_block, B), pltpu.VMEM(by_point, B),
            pltpu.VMEM((3 * C, N), B), pltpu.VMEM(by_channel, B), pltpu.VMEM(by_channel, F),
            pltpu.VMEM(by_channel, B), pltpu.VMEM(by_point, B), pltpu.VMEM(by_channel, B),
            pltpu.VMEM((3 * C, N), B), pltpu.VMEM(whole, F),
        ]
        + [pltpu.VMEM(half, B)] * 5
        + [pltpu.VMEM((PAIRS, OWNERS * PIECE, 128), B), pltpu.VMEM(whole, B)]
        + [pltpu.VMEM((2, N, N), B)]
        + [dma((2,))] * 8,
        collective_id=0,
    )(rank, feats, patch, gain, w_qkv, w_out, d_mixed)
    d_feats, g_qkv, g_out, g_gain, mixed = call(
        finish_kernel,
        [(by_point, B), ((C, 3 * C), F), ((C, C), F), ((1, C), F), (by_point, B)],
        8,
    )(code, ret, local, sums, tails, w_qkv, gain, mixed)
    return (mixed, d_feats, g_qkv, g_out, g_gain.reshape(C))


def solution(mesh):
    return jax.shard_map(
        on_device,
        mesh=mesh,
        in_specs=(
            P(("rep", "seq"), None),
            P(("rep", "seq")),
            P(("rep", "seq")),
            P(),
            P(),
            P(),
            P(("rep", "seq"), None),
        ),
        out_specs=(
            P(("rep", "seq"), None),
            P(("rep", "seq"), None),
            P("rep", None),
            P("rep", None),
            P("rep"),
        ),
        check_vma=False,
    )
```

```python
import functools

import jax
import jax.numpy as jnp
from jax import lax
from jax.experimental import pallas as pl
from jax.experimental.pallas import tpu as pltpu
from jax.sharding import PartitionSpec as P

F = jnp.float32
B = jnp.bfloat16
I = jnp.int32

N = 1024
C = 256
HDIM = 16
HEADS = C // HDIM
PEERS = 64
CAP = 4
SLOTS = PEERS * CAP
CHIPS = 32
WIDE = C // 2
PIECE = 16
HALF = CHIPS * PIECE
PAIR = 2 * HDIM
OWNERS = 16
PAIRS = 4
EPS = 1e-05
MASKED = 1e30
LOG2E = 1.4426950408889634
HALVES = 2
VMEM = 56 << 20

VECTOR = pl.BlockSpec(memory_space=pltpu.VMEM)


def dg(a, b, ca, cb):
    return lax.dot_general(a, b, (((ca,), (cb,)), ((), ())), preferred_element_type=F)


def iota(shape, dim):
    return lax.broadcasted_iota(I, shape, dim)


def greet():
    me = lax.axis_index("seq")
    barrier = pltpu.get_barrier_semaphore()

    def signal(step):
        peer = lax.rem(me + step, PEERS)
        pl.semaphore_signal(
            barrier, inc=1, device_id={"seq": peer}, device_id_type=pl.DeviceIdType.MESH
        )

    for step in range(1, PEERS):
        signal(step)


def met():
    pl.semaphore_wait(pltpu.get_barrier_semaphore(), PEERS - 1)


def remote(src, dst, send_sem, recv_sem, peer):
    return pltpu.make_async_remote_copy(
        src_ref=src,
        dst_ref=dst,
        send_sem=send_sem,
        recv_sem=recv_sem,
        device_id={"seq": peer},
        device_id_type=pl.DeviceIdType.MESH,
    )


def await_bytes(ref, sem):
    pltpu.make_async_copy(ref, ref, sem).wait()


def exchange(src, dst, send_sem, recv_sem):
    me = lax.axis_index("seq")

    def send(step):
        peer = lax.rem(me + step, PEERS)
        remote(src.at[peer], dst.at[me], send_sem, recv_sem, peer).start()

    for step in range(1, PEERS):
        send(step)


def await_exchange(ref, sem):
    await_bytes(ref.at[pl.ds(0, PEERS - 1)], sem)


def slot_rows(code):
    return (iota((SLOTS, 1), 0) == code).astype(F).astype(B)


def split(x):
    high = x.astype(B)
    return high, (x - high.astype(F)).astype(B)


def attention(q_ref, k_ref, v_ref, u_ref, group, att, gq, gk, gv, expo, after):
    one = jnp.where(group > 0, 1.0, 0.0)
    pad = jnp.zeros((HDIM - 2, N), F)
    q_bias = jnp.concatenate([-MASKED * (1 - one), -MASKED * one, pad], 0).astype(B)
    k_bias = jnp.concatenate([one, 1 - one, pad], 0).astype(B)
    ones = jnp.concatenate([jnp.ones((1, N), F), jnp.zeros((HDIM - 1, N), F)], 0).astype(B)
    scale = HDIM ** (-0.5)

    def rows_of(h):
        return pl.ds(pl.multiple_of(h * HDIM, HDIM), HDIM)

    def softmax_of(h, slot):
        rows = rows_of(h)
        q_high, q_low = split(q_ref[rows, :].astype(F) * (scale * LOG2E))
        query = jnp.concatenate([q_high, q_low, q_bias], 0)
        k = k_ref[rows, :]
        keys = jnp.concatenate([k, k, k_bias], 0).astype(F).T.astype(B)
        wide = N // (2 * HALVES)

        def block(b):
            span = slice(b * wide, (b + 1) * wide)
            scores = jnp.dot(keys, query[:, span], preferred_element_type=F)
            top = jnp.max(scores, axis=0, keepdims=True)
            expo[slot, :, span] = jnp.exp2(scores - top).astype(B)

        return block

    def head(h, slot, beside):
        rows = rows_of(h)
        k, v = k_ref[rows, :], v_ref[rows, :]
        q_wide, k_wide, v_wide = q_ref[rows, :].astype(F) * scale, k.astype(F), v.astype(F)
        u_wide = u_ref[rows, :].astype(F)
        center = jnp.mean(v_wide, axis=1, keepdims=True)
        v_wide = v_wide - center
        left = [v, ones, k] + [(v_wide[a : a + 1] * k_wide).astype(B) for a in range(HDIM)]
        left = jnp.concatenate(left, 0)
        wide = N // HALVES
        spans = [slice(b * wide, (b + 1) * wide) for b in range(HALVES)]
        right = []
        for b, span in enumerate(spans):
            beside(b)
            sums = jnp.dot(left, expo[slot, :, span], preferred_element_type=F)
            recip = 1.0 / sums[HDIM : HDIM + 1]
            attended = sums[:HDIM] * recip
            u = u_wide[:, span]
            delta = jnp.sum(u * (attended - center), axis=0, keepdims=True)
            grad = -delta * sums[2 * HDIM : 3 * HDIM]
            for a in range(HDIM):
                grad += u[a : a + 1] * sums[(3 + a) * HDIM : (4 + a) * HDIM]
            att[rows, span] = attended.astype(B)
            gq[rows, span] = (grad * (recip * scale)).astype(B)
            u = u * recip
            q = q_wide[:, span]
            parts = [u.astype(B), (q * (-delta * recip)).astype(B)]
            parts += [(u[a : a + 1] * q).astype(B) for a in range(HDIM)]
            right.append(jnp.concatenate(parts, 0))
        right = jnp.concatenate(right, 1)
        for b, span in enumerate(spans):
            beside(HALVES + b)
            sums = dg(right, expo[slot, span, :], 1, 1)
            grad = sums[HDIM : 2 * HDIM]
            for a in range(HDIM):
                grad += v_wide[a : a + 1, span] * sums[(2 + a) * HDIM : (3 + a) * HDIM]
            gv[rows, span] = sums[:HDIM].astype(B)
            gk[rows, span] = grad.astype(B)

    first = softmax_of(0, 0)
    for b in range(2 * HALVES):
        first(b)

    def heads(i, carry):
        head(2 * i, 0, softmax_of(2 * i + 1, 1))
        head(2 * i + 1, 1, softmax_of(2 * i + 2, 0))
        after(2 * i + 1)
        return carry

    lax.fori_loop(0, HEADS // 2 - 1, heads, 0)
    head(HEADS - 2, 0, softmax_of(HEADS - 1, 1))
    head(HEADS - 1, 1, lambda b: None)


def layer_kernel(
    rank_ref, feats_ref, patch_ref, gain_ref, w_qkv_ref, w_out_ref, d_mixed_ref,
    code_ref, mixed_ref, local_ref, ret_ref, sums_ref, tails_ref,
    send, got, flat, back_send, back_got,
    hil, qkv, up, normed, low, low_rows, att, gqkv, chunk,
    half_send, half_got, piece_send, piece_got, done, pair_send, pair_got, expo, d_mixed, come,
    go_sems, back_sems, half_sems, piece_sems, done_sems, last_sems, pair_sems, tail_sems,
):
    greet()
    me = lax.axis_index("seq")
    core = lax.rem(me, 2)
    chip = me // 2
    partner = chip * 2 + 1 - core
    own = pl.ds(pl.multiple_of(chip * PIECE, PIECE), PIECE)
    mine = pl.ds(pl.multiple_of(me * PIECE, PIECE), PIECE)
    others = pl.ds(0, (CHIPS - 1) * PIECE)
    peers = pl.ds(0, (PEERS - 1) * PIECE)

    rank = rank_ref[...]
    owner = rank // N
    onehot = (iota((PEERS, N), 0) == owner).astype(F)
    upto = (iota((N, N), 0) <= iota((N, N), 1)).astype(F).astype(B)
    count = jnp.dot(onehot.astype(B), upto, preferred_element_type=F)
    slot = jnp.sum(count * onehot, axis=0, keepdims=True).astype(I) - 1
    code = jnp.where(owner == me, -1, owner * CAP + slot)
    code_ref[...] = code
    chosen = slot_rows(code)
    spot = rank % N
    k = iota((128, N), 0)
    extra = jnp.where(k == 0, spot // 32, jnp.where(k == 1, spot % 32, jnp.where(k == 2, 1, 0)))
    rows = jnp.dot(chosen, feats_ref[...], preferred_element_type=F)
    spots = dg(chosen, extra.astype(F).astype(B), 1, 1)
    for o in range(PEERS):
        send[o, :, :C] = rows[o * CAP : (o + 1) * CAP].astype(B)
        send[o, :, C:] = spots[o * CAP : (o + 1) * CAP].astype(B)
    got[me] = jnp.zeros((CAP, C + 128), B)
    back_got[me] = jnp.zeros((CAP, C), B)
    met()
    exchange(send, got, go_sems.at[0], go_sems.at[1])

    here = jnp.where(owner == me, spot, -1)
    p = iota((N, 1), 0)
    stay = (p == here).astype(F).astype(B)
    hil[...] = jnp.dot(stay, feats_ref[...], preferred_element_type=F).astype(B)
    up[...] = dg(w_out_ref[...], d_mixed_ref[...], 1, 1).astype(B)
    gain = jnp.broadcast_to(gain_ref[...], (8, C)).T[:, :1]
    d_mixed[...] = d_mixed_ref[...].T
    await_exchange(got, go_sems.at[1])
    await_exchange(send, go_sems.at[0])

    for o in range(PEERS):
        flat[o * CAP : (o + 1) * CAP, :] = got[o].astype(F)
    spots = flat[:, C:].astype(B)
    weight = iota((16, 128), 1)
    weight = jnp.where(weight == 0, 32.0, jnp.where(weight < 2, 1.0, 0.0)).astype(B)
    valid = jnp.where(iota((16, 128), 1) == 2, 1.0, 0.0).astype(B)
    at = dg(weight, spots, 1, 1)[:1]
    at = jnp.where(dg(valid, spots, 1, 1)[:1] > 0.5, at, -1.0).astype(I)
    come[...] = (p == at).astype(F).astype(B)
    rows = hil[...].astype(F)
    rows += jnp.dot(come[...], flat[:, :C].astype(B), preferred_element_type=F)
    hil[...] = rows.astype(B)

    wide = rows.T
    centred = wide - jnp.mean(wide, axis=0, keepdims=True)
    recip = lax.rsqrt(jnp.mean(centred * centred, axis=0, keepdims=True) + EPS)
    normed[...] = centred * recip
    scaled = normed[...] * gain
    low[...] = scaled.astype(B)
    low_rows[...] = scaled.T.astype(B)
    qkv[...] = dg(w_qkv_ref[...], low[...], 0, 0).astype(B)

    def gradients(first, wide):
        parts = [gqkv[pl.ds(m * C + first, wide), :] for m in range(3)]
        sums = jnp.dot(jnp.concatenate(parts, 0), low_rows[...], preferred_element_type=F)
        sums = [sums[m * wide : (m + 1) * wide] for m in range(3)]
        span = pl.ds(first, wide)
        return sums + [jnp.dot(att[span, :], d_mixed_ref[...], preferred_element_type=F)]

    def start_sum():
        sums = gradients(0, WIDE)
        for m in range(4):
            for side in range(2):
                first = (m // 2) * HALF + side * 2 * WIDE + (m % 2) * WIDE
                chunk[first : first + WIDE, :] = sums[m][:, side * 128 : (side + 1) * 128]
        theirs = pl.ds(pl.multiple_of((1 - core) * HALF, HALF), HALF)
        half_send[...] = chunk[theirs, :].astype(B)
        remote(half_send, half_got, half_sems.at[0], half_sems.at[1], partner).start()

    def scatter_sum():
        await_bytes(half_got, half_sems.at[1])
        kept = chunk[pl.ds(pl.multiple_of(core * HALF, HALF), HALF), :]
        piece_send[...] = (kept + half_got[...].astype(F)).astype(B)
        piece_got[own, :] = piece_send[own, :]

        def scatter(step):
            to = lax.rem(chip + step, CHIPS)
            theirs = pl.ds(pl.multiple_of(to * PIECE, PIECE), PIECE)
            remote(
                piece_send.at[theirs], piece_got.at[own],
                piece_sems.at[0], piece_sems.at[1], to * 2 + core,
            ).start()

        for step in range(1, CHIPS):
            scatter(step)

    def total_of(pieces, count):
        total = pieces[0:PIECE, :].astype(F)
        for j in range(1, count):
            total += pieces[j * PIECE : (j + 1) * PIECE, :].astype(F)
        return total.astype(B)

    def gather_sum():
        await_bytes(piece_got.at[others], piece_sems.at[1])
        done[own, :] = total_of(piece_got, CHIPS)

        def gather(step):
            to = lax.rem(chip + step, CHIPS)
            remote(
                done.at[own], done.at[own], done_sems.at[0], done_sems.at[1], to * 2 + core
            ).start()

        for step in range(1, CHIPS):
            gather(step)

    def share_sum():
        await_bytes(done.at[others], done_sems.at[1])
        kept = pl.ds(pl.multiple_of(core * HALF, HALF), HALF)
        remote(done, sums_ref.at[kept], last_sems.at[0], last_sems.at[1], partner).start()
        sums_ref[kept, :] = done[...]

    def end_sum():
        await_bytes(done, last_sems.at[1])
        await_bytes(done, last_sems.at[0])
        await_bytes(half_send, half_sems.at[0])
        await_bytes(piece_send.at[others], piece_sems.at[0])
        await_bytes(done.at[others], done_sems.at[0])

    turn = lax.rem(me, PAIRS)

    def start_pair(c):
        sums = gradients(WIDE + c * PAIR if isinstance(c, int) else pl.multiple_of(WIDE + c * PAIR, PAIR), PAIR)
        for m in range(4):
            for side in range(2):
                first = (side * 4 + m) * PAIR
                pair_send[c, first : first + PAIR, :] = sums[m][
                    :, side * 128 : (side + 1) * 128
                ].astype(B)

        def piece(m):
            return pair_send.at[c, pl.ds(pl.multiple_of(m * PIECE, PIECE), PIECE)]

        def scatter(step):
            m = lax.rem(me // PAIRS + step, OWNERS)
            remote(
                piece(m), pair_got.at[mine], pair_sems.at[0], pair_sems.at[1], m * PAIRS + c
            ).start()

        @pl.when(turn == c)
        def _():
            pair_got[mine, :] = piece(me // PAIRS)[...]

        @pl.when(turn != c)
        def _():
            scatter(0)

        for step in range(1, OWNERS):
            scatter(step)

    def finish_pair():
        await_bytes(pair_got.at[peers], pair_sems.at[1])
        tails_ref[mine, :] = total_of(pair_got, PEERS)

        def gather(step):
            peer = lax.rem(me + step, PEERS)
            remote(
                tails_ref.at[mine], tails_ref.at[mine], tail_sems.at[0], tail_sems.at[1], peer
            ).start()

        for step in range(1, PEERS):
            gather(step)

    def after(h):
        for k, stage in enumerate((start_sum, scatter_sum, gather_sum, share_sum)):
            pl.when(h == HEADS // 2 - 1 + 2 * k)(stage)
        first = HEADS // 2 + 1
        pl.when(h >= first)(lambda: start_pair((h - first) // 2))

    patch = patch_ref[...]
    attention(
        qkv.at[:C], qkv.at[C : 2 * C], qkv.at[2 * C :], up,
        (patch == patch[:, :1]).astype(F),
        att, gqkv.at[:C], gqkv.at[C : 2 * C], gqkv.at[2 * C :], expo, after,
    )

    start_pair(PAIRS - 1)

    grad_normed = jnp.dot(w_qkv_ref[...], gqkv[...], preferred_element_type=F)
    scaled = grad_normed * gain
    d_norm = recip * (
        scaled
        - jnp.mean(scaled, axis=0, keepdims=True)
        - normed[...] * jnp.mean(scaled * normed[...], axis=0, keepdims=True)
    )
    d_rows = (d_mixed[...].astype(F) + d_norm).astype(B)
    back = jnp.dot(d_rows, come[...], preferred_element_type=F).T
    for o in range(PEERS):
        back_send[o] = back[o * CAP : (o + 1) * CAP].astype(B)
    exchange(back_send, back_got, back_sems.at[0], back_sems.at[1])
    finish_pair()
    stay = (p == here).astype(F).astype(B)
    local_ref[...] = jnp.dot(d_rows, stay, preferred_element_type=F).T.astype(B)
    mixed_ref[...] = (hil[...].astype(F) + dg(att[...], w_out_ref[...], 0, 0)).astype(B)
    end_sum()
    await_exchange(back_got, back_sems.at[1])
    await_exchange(back_send, back_sems.at[0])
    for o in range(PEERS):
        ret_ref[o * CAP : (o + 1) * CAP, :] = back_got[o]
    await_bytes(pair_got.at[peers], pair_sems.at[0])
    await_bytes(tails_ref.at[peers], tail_sems.at[1])
    await_bytes(tails_ref.at[peers], tail_sems.at[0])


def finish_kernel(
    code_ref, ret_ref, local_ref, sums_ref, tails_ref, w_qkv_ref, gain_ref, rows_ref,
    d_feats_ref, g_qkv_ref, g_out_ref, g_gain_ref, mixed_ref,
):
    mixed_ref[...] = rows_ref[...]
    d_feats = dg(slot_rows(code_ref[...]), ret_ref[...], 0, 0) + local_ref[...].astype(F)
    d_feats_ref[...] = d_feats.astype(B)

    def sums(m, side):
        first = (m // 2) * HALF + side * 2 * WIDE + (m % 2) * WIDE
        yield sums_ref[first : first + WIDE, :].astype(F)
        tails = []
        for c in range(PAIRS):
            for part in range(2):
                first = (((side * 4 + m) * 2 + part) * PAIRS + c) * PIECE
                tails.append(tails_ref[first : first + PIECE, :].astype(F))
        yield jnp.concatenate(tails, 0)

    for side in range(2):
        lanes = slice(side * 128, (side + 1) * 128)
        column = jnp.zeros((128, 128), F)
        for m in range(4):
            for g, part in enumerate(sums(m, side)):
                if m < 3:
                    at = slice(m * C + g * WIDE, m * C + (g + 1) * WIDE)
                    part = part.T
                    g_qkv_ref[lanes, at] = part
                    column += part * w_qkv_ref[lanes, at].astype(F)
                else:
                    g_out_ref[g * WIDE : (g + 1) * WIDE, lanes] = part
        total_row = jnp.sum(column.T, axis=0, keepdims=True)
        g_gain_ref[:, lanes] = total_row / gain_ref[:, lanes]


def call(kernel, out_shapes, n_in, scratch=(), collective_id=None):
    params = dict(vmem_limit_bytes=VMEM)
    if collective_id is not None:
        params.update(collective_id=collective_id, has_side_effects=True)
    return pl.pallas_call(
        kernel,
        out_shape=[jax.ShapeDtypeStruct(s, d) for s, d in out_shapes],
        in_specs=[VECTOR] * n_in,
        out_specs=[VECTOR] * len(out_shapes),
        scratch_shapes=list(scratch),
        compiler_params=pltpu.CompilerParams(**params),
    )


def on_device(feats, hilbert_rank, patch_id, gain, w_qkv, w_out, d_mixed):
    rank = hilbert_rank.reshape(1, N)
    patch = patch_id.reshape(1, N)
    gain = gain.reshape(1, C)
    dma = pltpu.SemaphoreType.DMA
    by_point, by_channel = (N, C), (C, N)
    half, whole = (HALF, 128), (2 * HALF, 128)
    out_block, back_block = (PEERS, CAP, C + 128), (PEERS, CAP, C)
    code, mixed, local, ret, sums, tails = call(
        layer_kernel,
        [((1, N), I), (by_point, B), (by_point, B), ((SLOTS, C), B), (whole, B), (whole, B)],
        7,
        [
            pltpu.VMEM(out_block, B), pltpu.VMEM(out_block, B), pltpu.VMEM((SLOTS, C + 128), F),
            pltpu.VMEM(back_block, B), pltpu.VMEM(back_block, B), pltpu.VMEM(by_point, B),
            pltpu.VMEM((3 * C, N), B), pltpu.VMEM(by_channel, B), pltpu.VMEM(by_channel, F),
            pltpu.VMEM(by_channel, B), pltpu.VMEM(by_point, B), pltpu.VMEM(by_channel, B),
            pltpu.VMEM((3 * C, N), B), pltpu.VMEM(whole, F),
        ]
        + [pltpu.VMEM(half, B)] * 5
        + [pltpu.VMEM((PAIRS, OWNERS * PIECE, 128), B), pltpu.VMEM(whole, B)]
        + [pltpu.VMEM((2, N, N), B), pltpu.VMEM(by_channel, B), pltpu.VMEM(by_point, B)]
        + [dma((2,))] * 8,
        collective_id=0,
    )(rank, feats, patch, gain, w_qkv, w_out, d_mixed)
    d_feats, g_qkv, g_out, g_gain, mixed = call(
        finish_kernel,
        [(by_point, B), ((C, 3 * C), F), ((C, C), F), ((1, C), F), (by_point, B)],
        8,
    )(code, ret, local, sums, tails, w_qkv, gain, mixed)
    return (mixed, d_feats, g_qkv, g_out, g_gain.reshape(C))


def solution(mesh):
    return jax.shard_map(
        on_device,
        mesh=mesh,
        in_specs=(
            P(("rep", "seq"), None),
            P(("rep", "seq")),
            P(("rep", "seq")),
            P(),
            P(),
            P(),
            P(("rep", "seq"), None),
        ),
        out_specs=(
            P(("rep", "seq"), None),
            P(("rep", "seq"), None),
            P("rep", None),
            P("rep", None),
            P("rep"),
        ),
        check_vma=False,
    )
```
